256 devices in a mesh: gz: 64 (over y_hi, z, x), gy: 4 (over y_lo, core).
Axes of the slice: x: 4, y: 4 (y_hi: 2, y_lo: 2; y = y_hi * 2 + y_lo), z: 8, core: 2. Of those that a mesh axis runs over, the one named last changes fastest.
Arguments:
- volume: float32 [256, 64, 2048], P('gz', 'gy'), may hold values from -10 to 10
- measured: float32 [64, 256, 2048], P('gz', None, 'gy'), may hold values from -48 to 48
- row_norm: float32 [64, 256, 2048], P('gz', None, 'gy'), may hold values from 4 to 40
- col_norm: float32 [256, 64, 2048], P('gz', 'gy'), may hold values from 8 to 800
- ray_weight: float32 [64, 64], P(None, 'gy'), may hold values from 0.5 to 1.5
- tiles: bfloat16 [16, 128, 128], replicated, may hold values from -0.5 to 0.5
- tile_kind: int32 [64, 16], replicated, may hold values from 0 to 15
- tile_band: int32 [64, 16], replicated, may hold values from 0 to 15, as said below
- band_start: int32 [64, 64], replicated, may hold values from 0 to 252, as said below
Outputs:
- smoothed: float32 [256, 64, 2048], P('gz', 'gy')
- residual: float32 [64, 256, 2048], P('gz', None, 'gy')
The draws below stay inside these ranges and needn't reach their ends.
Inputs may be any that keep to these rules, and one draw needn't show every extreme that they name: Plane k of slab s lands on detector row band_start + k; each entry lies within 2 rows of s * 4; slab 0 starts at row 0 and the last slab ends at the last row. `tile_band`: each entry lies within 2 of its x tile's own index; x tile 0 maps to detector tile 0 and the last x tile to the last detector tile.
All inputs are finite; a program needn't handle non-finite values.
Results may differ from the reference program's by a relative error of at most 0.0015.
Values may be sent and summed in bfloat16 or wider, within the bound.
No kernel may reach another device: no remote copies, remote signals or barrier semaphores. Data moves between devices by JAX's collectives and lax.ppermute only.
A program may use at most 192 MiB of HBM per device.

```python
import math
import jax
import jax.numpy as jnp
from jax import lax

NX = 2048
TILE = 128
NK = 16
PASSES = 3
Z_DEV = 4
Y_DEV = 16
NZ = 256
NY = 64
XT = 16
ANGLES = 64
N_GZ = 64
N_GY = 4


def plane_fraction():
    planes = jnp.arange(NZ, dtype=jnp.float32)
    return planes / jnp.float32(max(NZ - 1, 1))


def draw_volume(key, part):
    key = jax.random.fold_in(key, 5)
    frac = plane_fraction()[:, None, None]
    base = jnp.clip(jax.random.normal(key, (NZ, NY, NX), jnp.float32), -6.0, 6.0)
    scale = 0.02 * jnp.exp(jnp.log(75.0) * frac)
    return jnp.clip(base * scale, -10.0, 10.0).astype(jnp.float32)


def draw_col_norm(key, part):
    key = jax.random.fold_in(key, 9)
    frac = plane_fraction()[:, None, None]
    logs = jax.random.uniform(key, (NZ, NY, NX), jnp.float32, jnp.log(8.0), jnp.log(80.0))
    factor = jnp.exp(jnp.log(10.0) * (1.0 - frac))
    return jnp.clip(jnp.exp(logs) * factor, 8.0, 800.0).astype(jnp.float32)


def draw_band_start(key, part):
    key = jax.random.fold_in(key, 17)
    spread_rows = Z_DEV // 2
    offsets = jax.random.randint(key, (ANGLES, N_GZ), -spread_rows, spread_rows + 1)
    first_rows = jnp.arange(N_GZ, dtype=jnp.int32) * Z_DEV
    starts = jnp.clip(first_rows[None, :] + offsets, 0, Z_DEV * N_GZ - Z_DEV)
    starts = starts.at[:, 0].set(0)
    starts = starts.at[:, N_GZ - 1].set(Z_DEV * N_GZ - Z_DEV)
    return starts.astype(jnp.int32)


def draw_tile_band(key, part):
    key = jax.random.fold_in(key, 23)
    tile_count = NX // TILE
    shifts = jax.random.randint(key, (ANGLES, tile_count), -2, 3)
    tile_ids = jnp.arange(tile_count, dtype=jnp.int32)
    landing = jnp.clip(tile_ids[None, :] + shifts, 0, tile_count - 1)
    landing = landing.at[:, 0].set(0)
    landing = landing.at[:, tile_count - 1].set(tile_count - 1)
    return landing.astype(jnp.int32)


def place_ends(values, key, smallest, high):
    spot = [jax.random.randint(jax.random.fold_in(key, axis), (), 0, length) for axis, length in enumerate(values.shape)]
    longest = values.shape.index(max(values.shape))
    beside = spot[:longest] + [(spot[longest] + 1) % values.shape[longest]] + spot[longest + 1:]
    return values.at[tuple(spot)].set(smallest).at[tuple(beside)].set(high)


def steps_of(own_key, shape, shards, least, top_value):
    def one(dim, parts):
        heights = jax.random.uniform(jax.random.fold_in(jax.random.fold_in(own_key, 6), dim), (parts,), jnp.float32, least / len(shards), top_value / len(shards))
        return jnp.repeat(jnp.exp(heights), shape[dim] // parts).reshape((-1,) + (1,) * (len(shape) - dim - 1))

    gain = one(*shards[0])
    for cut in shards[1:]:
        gain = gain * one(*cut)
    return gain


def noise(stream_key, extent, deviation, most, pieces=(), kind=jnp.bfloat16):
    array = jax.random.normal(stream_key, extent, jnp.float32) * deviation
    if len(pieces) > 0:
        array = steps_of(stream_key, extent, pieces, -0.22, 0.18) * array
    return jnp.clip(array, min=-most, max=most).astype(kind)


def setup_inputs(seed: int = 0) -> dict:
    streams_of = jax.random.split(jax.random.key(seed), 10)
    return {
        "volume": draw_volume(jax.random.fold_in(streams_of[9], 71), 0),
        "measured": noise(streams_of[1], (ANGLES, NZ, NX), 8.0, 48.0, ((0, 64), (2, 4)), jnp.float32),
        "row_norm": jnp.clip(jnp.exp(math.log(40.0) - 2.3025851 * jax.random.uniform(streams_of[2], (ANGLES, NZ, NX), jnp.float32) ** steps_of(streams_of[2], (ANGLES, NZ, NX), ((0, 64), (2, 4)), -0.2, 0.2)), 4.0, 40.0),
        "col_norm": draw_col_norm(jax.random.fold_in(streams_of[9], 71), 0),
        "ray_weight": jnp.clip(0.5 + 1.0 * jax.random.uniform(streams_of[4], (ANGLES, NY), jnp.float32) ** steps_of(streams_of[4], (ANGLES, NY), ((1, 4),), -0.2, 0.2), 0.5, 1.5),
        "tiles": noise(streams_of[5], (NK, TILE, TILE), TILE ** -0.5, 0.5),
        "tile_kind": place_ends(jax.random.randint(streams_of[6], (ANGLES, XT), 0, NK), jax.random.fold_in(streams_of[6], 1), 0, NK - 1).astype(jnp.int32),
        "tile_band": draw_tile_band(jax.random.fold_in(streams_of[9], 71), 0),
        "band_start": draw_band_start(jax.random.fold_in(streams_of[9], 71), 0),
    }


EPS_TV = 0.01
EPS_NORM = 1e-06
RELAX = 1.0
TV_ALPHA = 0.2

def tv_gradient(volume_now):
    padded = jnp.pad(volume_now, 1)
    center = padded[1:-1, 1:-1, 1:-1]
    diff_z = padded[2:, 1:-1, 1:-1] - center
    diff_y = padded[1:-1, 2:, 1:-1] - center
    diff_x = padded[1:-1, 1:-1, 2:] - center
    magnitude = jnp.sqrt(diff_z * diff_z + diff_y * diff_y + diff_x * diff_x + EPS_TV)
    flux_z = diff_z / magnitude
    flux_y = diff_y / magnitude
    flux_x = diff_x / magnitude
    gradient = -(flux_z + flux_y + flux_x)
    gradient = gradient + jnp.pad(flux_z, ((1, 0), (0, 0), (0, 0)))[:-1]
    gradient = gradient + jnp.pad(flux_y, ((0, 0), (1, 0), (0, 0)))[:, :-1]
    gradient = gradient + jnp.pad(flux_x, ((0, 0), (0, 0), (1, 0)))[:, :, :-1]
    return gradient

def reference(volume, measured, row_norm, col_norm, ray_weight, tiles, tile_kind, tile_band, band_start):
    vol_blocks = volume.reshape(NZ, N_GY, Y_DEV, NX)
    row_ids = jnp.arange(NZ, dtype=jnp.int32)
    detector_tiles = jnp.arange(XT, dtype=jnp.int32)

    def per_angle(spread_sum, inputs):
        weight_row, tile_kinds, band_tiles, starts, measured_rows, row_scale = inputs
        weight_blocks = weight_row.reshape(N_GY, Y_DEV)
        ray_part = jnp.einsum('gy,zgyx->gzx', weight_blocks, vol_blocks, precision=lax.Precision.HIGHEST).astype(jnp.bfloat16)
        chosen = jnp.take(tiles, tile_kinds, axis=0).astype(jnp.float32)
        products = jnp.einsum('gzjc,jcd->gzjd', ray_part.astype(jnp.float32).reshape(N_GY, NZ, XT, TILE), chosen, precision=lax.Precision.HIGHEST)
        onehot = (band_tiles[:, None] == detector_tiles[None, :]).astype(jnp.float32)
        detector = jnp.einsum('gzjd,jt->ztd', products, onehot, precision=lax.Precision.HIGHEST).reshape(NZ, NX)
        landing = jnp.take(starts, row_ids // Z_DEV).astype(jnp.int32) + row_ids % Z_DEV
        placement = (row_ids[:, None] == landing[None, :]).astype(jnp.float32)
        projection = jnp.dot(placement, detector, precision=lax.Precision.HIGHEST)
        residual = (measured_rows - projection) / row_scale
        band_resid = jnp.dot(placement.T, residual, precision=lax.Precision.HIGHEST).astype(jnp.bfloat16)
        picked = jnp.take(band_resid.reshape(NZ, XT, TILE), band_tiles, axis=1).astype(jnp.float32)
        back_rows = jnp.einsum('zjc,jdc->zjd', picked, chosen, precision=lax.Precision.HIGHEST).reshape(NZ, NX)
        spread_sum = spread_sum + weight_row[None, :, None] * back_rows[:, None, :]
        return (spread_sum, residual)
    start_sum = jnp.zeros((NZ, NY, NX), jnp.float32)
    spread_sum, residual = lax.scan(per_angle, start_sum, (ray_weight, tile_kind, tile_band, band_start, measured, row_norm))
    updated = volume + RELAX * spread_sum / col_norm
    change = updated - volume
    moved = jnp.sqrt(jnp.sum(change * change))
    volume_now = updated
    for sweep in range(PASSES):
        gradient = tv_gradient(volume_now)
        grad_total = jnp.sqrt(jnp.sum(gradient * gradient) + EPS_NORM)
        volume_now = volume_now - TV_ALPHA * moved / grad_total * gradient
    return (volume_now, residual)
```

```python
import jax
import jax.numpy as jnp
from jax import lax
from jax.experimental import pallas as pl
from jax.experimental.pallas import tpu as pltpu
from jax.sharding import PartitionSpec as P

PASSES = 3
EPS_TV = 0.01
EPS_NORM = 1e-06
RELAX = 1.0
TV_ALPHA = 0.2

F32 = jnp.float32
BF16 = jnp.bfloat16
VMEM = pl.BlockSpec(memory_space=pltpu.VMEM)

PLANES, ROWS, HALO, TILE, XT, NK, ANGLES = 4, 16, 8, 128, 16, 16, 64
EXT = ROWS + HALO
WIDTH = XT * TILE
QUARTER = 4
WINDOW = 8
REACH = 10
SLOTS = 8


def iota(shape, dim):
    return lax.broadcasted_iota(jnp.int32, shape, dim)


def onehot(condition, dtype=F32):
    return jnp.where(condition, 1.0, 0.0).astype(dtype)


def dot(a, b, transposed=False):
    dims = (((1,), (1 if transposed else 0,)), ((), ()))
    return lax.dot_general(a, b, dims, preferred_element_type=F32)


def pieces(value, count):
    out = []
    for _ in range(count):
        part = value.astype(BF16)
        out.append(part)
        value = value - part.astype(F32)
    return out


def spread_lanes(parts, order):
    width = parts[0].shape[1]
    lanes = len(order) * width
    copy = onehot(iota((width, lanes), 1) % width == iota((width, lanes), 0), BF16)
    group = iota((parts[0].shape[0], lanes), 1) // width
    total = None
    for index, part in enumerate(parts):
        chosen = group == -1
        for place, which in enumerate(order):
            if which == index:
                chosen = chosen | (group == place)
        term = jnp.where(chosen, dot(part, copy), 0.0)
        total = term if total is None else total + term
    return total.astype(BF16)


def code_column(code, tile):
    lane = iota(code.shape, 1)
    column = jnp.sum(jnp.where(lane == tile, code, 0.0), axis=1, keepdims=True)
    return jnp.broadcast_to(column.astype(jnp.int32), (code.shape[0], TILE))


def slot_masks(kind):
    return [onehot((kind % SLOTS) == k, BF16) for k in range(SLOTS)]


def pick_half(wide, kind):
    return jnp.where(kind >= SLOTS, wide[:, TILE:], wide[:, :TILE])


def project_kernel(
    own, near, far, farnear, w_own, w_near, kinds, bands, tiles, out, weights_out,
    sums, lhs, rhs, acc,
):
    block = lax.axis_index("gy")
    core = block % 2
    first = block * 2 + jnp.where(block >= 2, 2, 0)
    start = pl.multiple_of(first * TILE, TILE)
    inner = pl.multiple_of(core * 2 * TILE, TILE)
    span = WINDOW * TILE
    w_far = far[:, REACH * TILE : (REACH + 1) * TILE][:, :ROWS]
    w_farnear = farnear[:, REACH * TILE : (REACH + 1) * TILE][:, :ROWS]
    sources = (
        (own, start, w_own[...], 0),
        (near, start, w_near[...], 1),
        (far, inner, w_far, 2),
        (farnear, inner, w_farnear, 3),
    )
    row = iota((EXT, ROWS), 0)
    wanted = block * ROWS + row - jnp.where(row >= ROWS + HALO // 2, EXT, 0)
    picked = jnp.zeros((EXT, ANGLES), F32)
    for order, (ref, offset, weight, flip) in enumerate(sources):
        w_parts = pieces(weight, 3)
        left = spread_lanes(w_parts, (0, 0, 1, 1, 0, 2))
        held = (block ^ flip) * ROWS + iota((EXT, ROWS), 1)
        choose = onehot(held == wanted, BF16)
        for part in w_parts:
            picked = picked + dot(choose, part, transposed=True)
        for z in range(PLANES):
            v = pieces(ref[z * ROWS : (z + 1) * ROWS, pl.ds(offset, span)], 3)
            right = jnp.concatenate([v[0], v[1], v[0], v[1], v[2], v[0]], axis=0)
            rays = dot(left, right).astype(BF16).astype(F32)
            here = sums.at[z * ANGLES : (z + 1) * ANGLES, :]
            here[...] = rays if order == 0 else here[...] + rays
    weights_out[...] = picked
    for k in range(SLOTS):
        rhs[k * TILE : (k + 1) * TILE, :TILE] = tiles[k]
        rhs[k * TILE : (k + 1) * TILE, TILE:] = tiles[k + SLOTS]
    acc[...] = jnp.zeros_like(acc)
    code = (kinds[...] + NK * bands[...]).astype(F32)
    rows = PLANES * ANGLES
    for j in range(WINDOW):
        column = code_column(code, first + j)
        kind, band = column % NK, column // NK
        masks = slot_masks(kind)
        for z in range(PLANES):
            part = sums[z * ANGLES : (z + 1) * ANGLES, j * TILE : (j + 1) * TILE]
            for p, piece in enumerate(pieces(part, 2)):
                at = (p * PLANES + z) * ANGLES
                for k in range(SLOTS):
                    lhs[at : at + ANGLES, k * TILE : (k + 1) * TILE] = piece * masks[k]
        wide = dot(lhs[...], rhs[...])
        wide = wide[:rows] + wide[rows:]
        for z in range(PLANES):
            tile = pick_half(wide[z * ANGLES : (z + 1) * ANGLES], kind)
            for t in range(QUARTER):
                here = acc.at[t, z * ANGLES : (z + 1) * ANGLES, :]
                here[...] += jnp.where(band == block * QUARTER + t, tile, 0.0)
    for t in range(QUARTER):
        for z in range(PLANES):
            out[pl.ds(t * PLANES + z, ANGLES, stride=XT), :] = acc[
                t, z * ANGLES : (z + 1) * ANGLES, :
            ]


def residual_kernel(rows_in, measured, norm, starts, resid, band_out, gathered, placed):
    angle = lax.axis_index("gz")
    slabs = starts.shape[1]
    total = PLANES * slabs
    mine = jnp.where(iota(starts.shape, 0) == angle, starts[...], 0).astype(F32)
    first = jnp.sum(mine, axis=0, keepdims=True)
    spread = onehot(iota((slabs, total), 1) % slabs == iota((slabs, total), 0), BF16)
    land = dot(jnp.broadcast_to(first, (8, slabs)).astype(BF16), spread)[:1]
    land = land.astype(jnp.int32) + iota((1, total), 1) // slabs
    place = onehot(iota((total, total), 0) == land, BF16)
    r = iota((total, slabs), 0)
    own = jnp.where(r % slabs == iota((total, slabs), 1), first, 0.0)
    land_col = jnp.sum(own, axis=1, keepdims=True).astype(jnp.int32)
    land_col = land_col + iota((total, 1), 0) // slabs
    take = onehot(iota((total, total), 1) == land_col, BF16)
    for t in range(QUARTER):
        for z in range(PLANES):
            gathered[z * slabs : (z + 1) * slabs, t * TILE : (t + 1) * TILE] = rows_in[
                pl.ds(t * PLANES + z, slabs, stride=XT), :
            ]
    projection = None
    for part in pieces(gathered[...], 3):
        term = dot(place, part)
        projection = term if projection is None else projection + term
    residual = (measured[...] - projection) / norm[...]
    resid[...] = residual
    rows = dot(take, residual.astype(BF16))
    for t in range(QUARTER):
        for z in range(PLANES):
            placed[pl.ds(t * PLANES + z, slabs, stride=XT), :] = rows[
                z * slabs : (z + 1) * slabs, t * TILE : (t + 1) * TILE
            ]
    band_out[...] = placed[...].astype(BF16)


def inside_rows(block):
    row = iota((EXT, 1), 0)
    y = block * ROWS + row - jnp.where(row >= ROWS + HALO // 2, EXT, 0)
    return (y >= 0) & (y < lax.axis_size("gy") * ROWS)


def back_kernel(
    band0, band1, band2, band3, kinds, bands, tiles, weights, volume, norm, after, before,
    updated, first_plane, last_plane, moved, flat, rows_by_tile, lhs, rhs,
):
    block = lax.axis_index("gy")
    for flip, ref in enumerate((band0, band1, band2, band3)):
        flat[...] = ref[...].astype(F32)
        for t in range(QUARTER):
            for z in range(PLANES):
                rows_by_tile[(block ^ flip) * QUARTER + t, z * ANGLES : (z + 1) * ANGLES, :] = (
                    flat[pl.ds(t * PLANES + z, ANGLES, stride=XT), :].astype(BF16)
                )
    for k in range(SLOTS):
        rhs[k * TILE : (k + 1) * TILE, :TILE] = tiles[k]
        rhs[k * TILE : (k + 1) * TILE, TILE:] = tiles[k + SLOTS]
    left = spread_lanes(pieces(weights[...], 2), (0, 0, 1))
    code = (kinds[...] + NK * bands[...]).astype(F32)
    inside = inside_rows(block)
    low = iota((HALO, 2 * TILE), 0) < HALO // 2
    squares = jnp.zeros((ROWS, 2 * TILE), F32)
    for pair in range(XT // 2):
        backs = []
        for j in (2 * pair, 2 * pair + 1):
            column = code_column(code, j)
            kind, band = column % NK, column // NK
            masks = slot_masks(kind)
            near = [t for t in range(j - 2, j + 3) if 0 <= t < XT]
            at_band = [onehot(band == t, BF16) for t in near]
            for z in range(PLANES):
                here = slice(z * ANGLES, (z + 1) * ANGLES)
                chosen = None
                for t, mask in zip(near, at_band):
                    term = rows_by_tile[t, here, :] * mask
                    chosen = term if chosen is None else chosen + term
                for k in range(SLOTS):
                    lhs[here, k * TILE : (k + 1) * TILE] = chosen * masks[k]
            wide = dot(lhs[...], rhs[...])
            backs.append(
                [pick_half(wide[z * ANGLES : (z + 1) * ANGLES], kind) for z in range(PLANES)]
            )
        lanes = slice(2 * pair * TILE, (2 * pair + 2) * TILE)
        for z in range(PLANES):
            back = jnp.concatenate([backs[0][z], backs[1][z]], axis=1)
            b = pieces(back, 2)
            smeared = dot(left, jnp.concatenate([b[0], b[1], b[0]], axis=0))
            up, down = after[z, :, lanes], before[z, :, lanes]
            v = jnp.concatenate(
                [volume[z, :, lanes], jnp.where(low, up, pltpu.roll(down, HALO // 2, 0))], axis=0
            )
            n = jnp.concatenate(
                [norm[z, :, lanes], jnp.where(low, pltpu.roll(up, HALO // 2, 0), down)], axis=0
            )
            new = v + RELAX * smeared / jnp.where(inside, n, 1.0)
            updated[z, :, lanes] = new
            if z == 0:
                first_plane[0, :, lanes] = new
            if z == PLANES - 1:
                last_plane[0, :, lanes] = new
            change = (new - v)[:ROWS]
            squares = squares + change * change
    total = jnp.sum(squares, axis=(0, 1), keepdims=True)
    moved[...] = jnp.where(iota((8, TILE), 1) == 0, total, 0.0)


def gradient_plane(here, above, flux_z_below, inside):
    lane = iota(here.shape, 1)
    ahead = jnp.where(lane == WIDTH - 1, 0.0, pltpu.roll(here, WIDTH - 1, 1))
    dz = above - here
    dy = pltpu.roll(here, EXT - 1, 0) - here
    dx = ahead - here
    scale = lax.rsqrt(dz * dz + dy * dy + dx * dx + EPS_TV)
    scale = jnp.where(inside, scale, 0.0)
    qz, qy, qx = dz * scale, dy * scale, dx * scale
    gradient = flux_z_below - (qz + qy + qx)
    gradient = gradient + pltpu.roll(qy, 1, 0)
    gradient = gradient + jnp.where(lane == 0, 0.0, pltpu.roll(qx, 1, 1))
    return jnp.where(inside, gradient, 0.0), qz


def flux_below(below, here, inside):
    lane = iota(here.shape, 1)
    ahead = jnp.where(lane == WIDTH - 1, 0.0, pltpu.roll(below, WIDTH - 1, 1))
    dz = here - below
    dy = pltpu.roll(below, EXT - 1, 0) - below
    dx = ahead - below
    scale = lax.rsqrt(dz * dz + dy * dy + dx * dx + EPS_TV)
    return jnp.where(inside, dz * scale, 0.0)


def write_gradients(planes, moved, grad, grad_first, grad_last, parts):
    inside = inside_rows(lax.axis_index("gy"))
    exists = inside & (lax.axis_index("gz") > 0)
    flux = flux_below(planes(0), planes(1), exists)
    squares = jnp.zeros((ROWS, WIDTH), F32)
    for z in range(PLANES):
        g, flux = gradient_plane(planes(z + 1), planes(z + 2), flux, inside)
        grad[z] = g
        if z == 0:
            grad_first[0] = g
        if z == PLANES - 1:
            grad_last[0] = g
        squares = squares + g[:ROWS] * g[:ROWS]
    total = jnp.sum(squares, axis=(0, 1), keepdims=True)
    row = moved[:1] + jnp.where(iota((1, TILE), 1) == 1, total, 0.0)
    parts[...] = jnp.broadcast_to(row, parts.shape)


def first_gradient_kernel(f, below, above, moved, grad, grad_first, grad_last, parts):
    def planes(i):
        return below[0] if i == 0 else above[0] if i == PLANES + 1 else f[i - 1]

    write_gradients(planes, moved, grad, grad_first, grad_last, parts)


def step_length(sums):
    row = jnp.sum(sums[...], axis=0, keepdims=True)
    lane = iota(row.shape, 1)
    moved = jnp.sum(jnp.where(lane == 0, row, 0.0), axis=1, keepdims=True)
    total = jnp.sum(jnp.where(lane == 1, row, 0.0), axis=1, keepdims=True)
    return TV_ALPHA * jnp.sqrt(moved) / jnp.sqrt(total + EPS_NORM)


def next_gradient_kernel(
    sums, f, below, above, g, g_below, g_above, moved,
    f_out, below_out, above_out, grad, grad_first, grad_last, parts,
):
    step = step_length(sums)
    below_out[0] = below[0] - step * g_below[0]
    above_out[0] = above[0] - step * g_above[0]
    for z in range(PLANES):
        f_out[z] = f[z] - step * g[z]

    def planes(i):
        return below_out[0] if i == 0 else above_out[0] if i == PLANES + 1 else f_out[i - 1]

    write_gradients(planes, moved, grad, grad_first, grad_last, parts)


def last_step_kernel(sums, f, g, out):
    step = step_length(sums)
    for z in range(PLANES):
        out[z] = f[z, :ROWS] - step * g[z, :ROWS]


def call(kernel, shapes, args, scratch=(), flops=0):
    shapes = [jax.ShapeDtypeStruct(shape, dtype) for shape, dtype in shapes]
    moved = sum(a.size * a.dtype.itemsize for a in list(args) + shapes)
    out = pl.pallas_call(
        kernel,
        out_shape=shapes,
        in_specs=[VMEM] * len(args),
        out_specs=[VMEM] * len(shapes),
        scratch_shapes=list(scratch),
        compiler_params=pltpu.CompilerParams(vmem_limit_bytes=40 * 1024 * 1024),
        cost_estimate=pl.CostEstimate(flops=flops, bytes_accessed=moved, transcendentals=0),
    )(*args)
    return out


def per_device(
    volume, measured, row_norm, col_norm, ray_weight, tiles, tile_kind, tile_band, band_start
):
    slabs, blocks = lax.axis_size("gz"), lax.axis_size("gy")
    block = lax.axis_index("gy")
    other_chip = [(i, i ^ 2) for i in range(blocks)]
    other_core = [(i, i ^ 1) for i in range(blocks)]
    flat = volume.reshape(PLANES * ROWS, WIDTH)
    away = jnp.where(block >= 2, 0, (XT - REACH) * TILE)
    lanes = jnp.pad(ray_weight, ((0, 0), (0, TILE - ROWS)))
    outgoing = lax.dynamic_slice_in_dim(flat, away, REACH * TILE, axis=1)
    far = lax.ppermute(jnp.concatenate([outgoing, lanes], axis=1), "gy", other_chip)
    near = lax.ppermute(flat, "gy", other_core)
    w_near = lax.ppermute(ray_weight, "gy", other_core)
    farnear = lax.ppermute(far, "gy", other_core)
    half = HALO // 2
    to_before = jnp.concatenate([volume[:, :half], col_norm[:, :half]], axis=1)
    to_after = jnp.concatenate([volume[:, ROWS - half :], col_norm[:, ROWS - half :]], axis=1)
    after = lax.ppermute(to_before, "gy", [(i + 1, i) for i in range(blocks - 1)])
    before = lax.ppermute(to_after, "gy", [(i, i + 1) for i in range(blocks - 1)])

    rows = PLANES * ANGLES
    chunk = ANGLES * QUARTER * PLANES
    slab_proj, weights = call(
        project_kernel,
        [((chunk, TILE), F32), ((EXT, ANGLES), F32)],
        (flat, near, far, farnear, ray_weight, w_near, tile_kind, tile_band, tiles),
        [
            pltpu.VMEM((rows, WINDOW * TILE), F32),
            pltpu.VMEM((2 * rows, SLOTS * TILE), BF16),
            pltpu.VMEM((SLOTS * TILE, 2 * TILE), BF16),
            pltpu.VMEM((QUARTER, rows, TILE), F32),
        ],
        flops=2 * WINDOW * 2 * rows * SLOTS * TILE * 2 * TILE,
    )
    chunks = slab_proj.reshape(slabs, XT, TILE)
    owner_rows = lax.all_to_all(chunks, "gz", split_axis=0, concat_axis=0, tiled=True)
    residual, band_resid = call(
        residual_kernel,
        [(measured.shape[1:], F32), ((chunk, TILE), BF16)],
        (owner_rows.reshape(chunk, TILE), measured[0], row_norm[0], band_start),
        [pltpu.VMEM((rows, QUARTER * TILE), F32), pltpu.VMEM((chunk, TILE), F32)],
        flops=2 * 4 * rows * rows * QUARTER * TILE,
    )
    chunks = band_resid.reshape(slabs, XT, TILE)
    bands = lax.all_to_all(chunks, "gz", split_axis=0, concat_axis=0, tiled=True)
    bands = bands.reshape(chunk, TILE)
    bands_far = lax.ppermute(bands, "gy", other_chip)
    bands_near = lax.ppermute(bands, "gy", other_core)
    bands_farnear = lax.ppermute(bands_far, "gy", other_core)

    plane = ((1, EXT, WIDTH), F32)
    block_ext = ((PLANES, EXT, WIDTH), F32)
    f, f_first, f_last, moved = call(
        back_kernel,
        [block_ext, plane, plane, ((8, TILE), F32)],
        (
            bands, bands_near, bands_far, bands_farnear, tile_kind, tile_band,
            jnp.swapaxes(tiles, 1, 2), weights, volume, col_norm, after, before,
        ),
        [
            pltpu.VMEM((chunk, TILE), F32),
            pltpu.VMEM((XT, rows, TILE), BF16),
            pltpu.VMEM((rows, SLOTS * TILE), BF16),
            pltpu.VMEM((SLOTS * TILE, 2 * TILE), BF16),
        ],
        flops=2 * XT * rows * SLOTS * TILE * 2 * TILE,
    )
    upward = [(i, i + 1) for i in range(slabs - 1)]
    downward = [(i + 1, i) for i in range(slabs - 1)]

    def neighbours(first, last):
        return lax.ppermute(last, "gz", upward), lax.ppermute(first, "gz", downward)

    def summed(parts):
        return lax.all_to_all(parts, ("gz", "gy"), split_axis=0, concat_axis=0, tiled=True)

    partial = ((slabs * blocks, TILE), F32)
    work = 40 * PLANES * EXT * WIDTH
    below, above = neighbours(f_first, f_last)
    g, g_first, g_last, parts = call(
        first_gradient_kernel,
        [block_ext, plane, plane, partial],
        (f, below, above, moved),
        flops=work,
    )
    for _ in range(PASSES - 1):
        g_below, g_above = neighbours(g_first, g_last)
        sums = summed(parts)
        f, below, above, g, g_first, g_last, parts = call(
            next_gradient_kernel,
            [block_ext, plane, plane, block_ext, plane, plane, partial],
            (sums, f, below, above, g, g_below, g_above, moved),
            flops=work,
        )
    (smoothed,) = call(
        last_step_kernel,
        [(volume.shape, F32)],
        (summed(parts), f, g),
        flops=2 * volume.size,
    )
    return smoothed, residual[None]


def solution(mesh):
    placed = (
        P("gz", "gy", None),
        P("gz", None, "gy"),
        P("gz", None, "gy"),
        P("gz", "gy", None),
        P(None, "gy"),
        P(),
        P(),
        P(),
        P(),
    )
    return jax.shard_map(
        per_device,
        mesh=mesh,
        in_specs=placed,
        out_specs=(P("gz", "gy", None), P("gz", None, "gy")),
        check_vma=False,
    )
```

```python
import jax
import jax.numpy as jnp
from jax import lax
from jax.experimental import pallas as pl
from jax.experimental.pallas import tpu as pltpu
from jax.sharding import PartitionSpec as P

PASSES = 3
EPS_TV = 0.01
EPS_NORM = 1e-06
RELAX = 1.0
TV_ALPHA = 0.2

F32 = jnp.float32
BF16 = jnp.bfloat16
VMEM = pl.BlockSpec(memory_space=pltpu.VMEM)

PLANES, ROWS, HALO, TILE, XT, NK, ANGLES = 4, 16, 8, 128, 16, 16, 64
EXT = ROWS + HALO
WIDTH = XT * TILE
QUARTER = 4
WINDOW = 8
REACH = 10
SLOTS = 8


def iota(shape, dim):
    return lax.broadcasted_iota(jnp.int32, shape, dim)


def onehot(condition, dtype=F32):
    return jnp.where(condition, 1.0, 0.0).astype(dtype)


def dot(a, b, transposed=False):
    dims = (((1,), (1 if transposed else 0,)), ((), ()))
    return lax.dot_general(a, b, dims, preferred_element_type=F32)


def pieces(value, count):
    out = []
    for _ in range(count):
        part = value.astype(BF16)
        out.append(part)
        value = value - part.astype(F32)
    return out


def spread_lanes(parts, order, first, width):
    rows, held = parts[0].shape
    lanes = len(order) * width
    copy = onehot(iota((held, lanes), 1) % width + first == iota((held, lanes), 0), BF16)
    group = iota((rows, lanes), 1) // width
    total = None
    for index, part in enumerate(parts):
        chosen = group == -1
        for place, which in enumerate(order):
            if which == index:
                chosen = chosen | (group == place)
        term = jnp.where(chosen, dot(part, copy), 0.0)
        total = term if total is None else total + term
    return total.astype(BF16)


def start_fetches(pairs, arrived):
    fetches = [
        pltpu.make_async_copy(there, here, arrived.at[i]) for i, (there, here) in enumerate(pairs)
    ]
    for fetch in fetches:
        fetch.start()
    return fetches


def code_column(code, tile):
    lane = iota(code.shape, 1)
    column = jnp.sum(jnp.where(lane == tile, code, 0.0), axis=1, keepdims=True)
    return jnp.broadcast_to(column.astype(jnp.int32), (code.shape[0], TILE))


def slot_masks(kind):
    return [onehot((kind % SLOTS) == k, BF16) for k in range(SLOTS)]


def pick_half(wide, kind):
    return jnp.where(kind >= SLOTS, wide[:, TILE:], wide[:, :TILE])


def project_kernel(
    far, farnear, near, small, own, tiles, out, weights_out,
    own_here, sums, lhs, rhs, acc, arrived,
):
    block = lax.axis_index("gy")
    first = block * 2 + jnp.where(block >= 2, 2, 0)
    span = WINDOW * TILE
    window = pl.ds(pl.multiple_of(first * TILE, TILE), span)
    inner = pl.ds(pl.multiple_of(block % 2 * 2 * TILE, TILE), span)
    fetches = start_fetches(
        (
            (own.at[:, window], own_here),
            (tiles.at[:SLOTS], rhs.at[:, :, :TILE]),
            (tiles.at[SLOTS:], rhs.at[:, :, TILE:]),
        ),
        arrived,
    )
    acc[...] = jnp.zeros_like(acc)
    sources = ((far, 2, inner), (farnear, 3, inner), (near, 1, slice(0, span)), (own_here, 0, slice(0, span)))
    weight = [ref[:ROWS, ref.shape[1] - TILE :][:, :ANGLES] for ref in (far, farnear, near)]
    weight = pieces(jnp.concatenate([*weight, small[XT:]], axis=0).T, 3)
    row = iota((EXT, 1), 0)
    wanted = block * ROWS + row - jnp.where(row >= ROWS + HALO // 2, EXT, 0)
    lane = iota((EXT, ANGLES), 1)
    held_row = jnp.zeros((EXT, ANGLES), jnp.int32)
    for order, (_, flip, _) in enumerate(sources):
        mine = lane // ROWS == order
        held_row = held_row + jnp.where(mine, (block ^ flip) * ROWS + lane % ROWS, 0)
    choose = onehot(held_row == wanted, BF16)
    picked = jnp.zeros((EXT, ANGLES), F32)
    for part in weight:
        picked = picked + dot(choose, part, transposed=True)
    for order, (ref, _, lanes) in enumerate(sources):
        if order == 3:
            fetches[0].wait()
        left = spread_lanes(weight, (0, 0, 1, 1, 0, 2), order * ROWS, ROWS)
        for z in range(PLANES):
            v = pieces(ref[z * ROWS : (z + 1) * ROWS, lanes], 3)
            right = jnp.concatenate([v[0], v[1], v[0], v[1], v[2], v[0]], axis=0)
            rays = dot(left, right).astype(BF16).astype(F32)
            here = sums.at[z * ANGLES : (z + 1) * ANGLES, :]
            here[...] = rays if order == 0 else here[...] + rays
    weights_out[...] = picked
    for fetch in fetches[1:]:
        fetch.wait()
    code = small[:XT].T
    rows = PLANES * ANGLES
    for j in range(WINDOW):
        column = code_column(code, first + j)
        kind, band = column % NK, column // NK
        masks = slot_masks(kind)
        for z in range(PLANES):
            part = sums[z * ANGLES : (z + 1) * ANGLES, j * TILE : (j + 1) * TILE]
            for p, piece in enumerate(pieces(part, 2)):
                at = (p * PLANES + z) * ANGLES
                for k in range(SLOTS):
                    lhs[at : at + ANGLES, k * TILE : (k + 1) * TILE] = piece * masks[k]
        wide = dot(lhs[...], rhs[...].reshape(SLOTS * TILE, 2 * TILE))
        wide = wide[:rows] + wide[rows:]
        for z in range(PLANES):
            tile = pick_half(wide[z * ANGLES : (z + 1) * ANGLES], kind)
            for t in range(QUARTER):
                here = acc.at[t, z * ANGLES : (z + 1) * ANGLES, :]
                here[...] += jnp.where(band == block * QUARTER + t, tile, 0.0)
    for t in range(QUARTER):
        for z in range(PLANES):
            out[pl.ds(t * PLANES + z, ANGLES, stride=XT), :] = acc[
                t, z * ANGLES : (z + 1) * ANGLES, :
            ]


def residual_kernel(rows_in, measured, norm, starts, resid, band_out, gathered, placed):
    angle = lax.axis_index("gz")
    slabs = starts.shape[1]
    total = PLANES * slabs
    mine = jnp.where(iota(starts.shape, 0) == angle, starts[...], 0).astype(F32)
    first = jnp.sum(mine, axis=0, keepdims=True)
    spread = onehot(iota((slabs, total), 1) % slabs == iota((slabs, total), 0), BF16)
    land = dot(jnp.broadcast_to(first, (8, slabs)).astype(BF16), spread)[:1]
    land = land.astype(jnp.int32) + iota((1, total), 1) // slabs
    place = onehot(iota((total, total), 0) == land, BF16)
    r = iota((total, slabs), 0)
    own = jnp.where(r % slabs == iota((total, slabs), 1), first, 0.0)
    land_col = jnp.sum(own, axis=1, keepdims=True).astype(jnp.int32)
    land_col = land_col + iota((total, 1), 0) // slabs
    take = onehot(iota((total, total), 1) == land_col, BF16)
    for t in range(QUARTER):
        for z in range(PLANES):
            gathered[z * slabs : (z + 1) * slabs, t * TILE : (t + 1) * TILE] = rows_in[
                pl.ds(t * PLANES + z, slabs, stride=XT), :
            ]
    projection = None
    for part in pieces(gathered[...], 3):
        term = dot(place, part)
        projection = term if projection is None else projection + term
    residual = (measured[...] - projection) / norm[...]
    resid[...] = residual
    rows = dot(take, residual.astype(BF16))
    for t in range(QUARTER):
        for z in range(PLANES):
            placed[pl.ds(t * PLANES + z, slabs, stride=XT), :] = rows[
                z * slabs : (z + 1) * slabs, t * TILE : (t + 1) * TILE
            ]
    band_out[...] = placed[...].astype(BF16)


def inside_rows(block):
    row = iota((EXT, 1), 0)
    y = block * ROWS + row - jnp.where(row >= ROWS + HALO // 2, EXT, 0)
    return (y >= 0) & (y < lax.axis_size("gy") * ROWS)


def back_kernel(
    b0, b1, b2, b3, small, weights, tiles, volume, norm, after, before,
    updated, first_planes, last_planes, moved,
    flat, rows_by_tile, lhs, rhs,
    volume_here, norm_here, after_here, before_here, arrived,
):
    block = lax.axis_index("gy")
    fetches = start_fetches(
        (
            (tiles.at[:SLOTS], rhs.at[:, :, :TILE]),
            (tiles.at[SLOTS:], rhs.at[:, :, TILE:]),
            (volume, volume_here),
            (norm, norm_here),
            (after, after_here),
            (before, before_here),
        ),
        arrived,
    )
    left = spread_lanes(pieces(weights[...], 2), (0, 0, 1), 0, ANGLES)

    def arrange(flip, ref):
        flat[...] = ref[...].astype(F32)
        for t in range(QUARTER):
            for z in range(PLANES):
                rows_by_tile[(block ^ flip) * QUARTER + t, z * ANGLES : (z + 1) * ANGLES, :] = (
                    flat[pl.ds(t * PLANES + z, ANGLES, stride=XT), :].astype(BF16)
                )

    for flip, ref in enumerate((b0, b1, b2, b3)):
        arrange(flip, ref)
    for fetch in fetches:
        fetch.wait()
    code = small[:XT].T
    inside = inside_rows(block)
    low = iota((HALO, 2 * TILE), 0) < HALO // 2
    squares = jnp.zeros((ROWS, 2 * TILE), F32)
    for pair in range(XT // 2):
        backs = []
        for j in (2 * pair, 2 * pair + 1):
            column = code_column(code, j)
            kind, band = column % NK, column // NK
            masks = slot_masks(kind)
            near = [t for t in range(j - 2, j + 3) if 0 <= t < XT]
            at_band = [onehot(band == t, BF16) for t in near]
            for z in range(PLANES):
                here = slice(z * ANGLES, (z + 1) * ANGLES)
                chosen = None
                for t, mask in zip(near, at_band):
                    term = rows_by_tile[t, here, :] * mask
                    chosen = term if chosen is None else chosen + term
                for k in range(SLOTS):
                    lhs[here, k * TILE : (k + 1) * TILE] = chosen * masks[k]
            wide = dot(lhs[...], rhs[...].reshape(SLOTS * TILE, 2 * TILE))
            backs.append(
                [pick_half(wide[z * ANGLES : (z + 1) * ANGLES], kind) for z in range(PLANES)]
            )
        cut = slice(2 * pair * TILE, (2 * pair + 2) * TILE)
        for z in range(PLANES):
            back = jnp.concatenate([backs[0][z], backs[1][z]], axis=1)
            b = pieces(back, 2)
            smeared = dot(left, jnp.concatenate([b[0], b[1], b[0]], axis=0))
            up, down = after_here[z, :, cut], before_here[z, :, cut]
            v = jnp.concatenate(
                [volume_here[z, :, cut], jnp.where(low, up, pltpu.roll(down, HALO // 2, 0))], axis=0
            )
            n = jnp.concatenate(
                [norm_here[z, :, cut], jnp.where(low, pltpu.roll(up, HALO // 2, 0), down)], axis=0
            )
            new = v + RELAX * smeared / jnp.where(inside, n, 1.0)
            updated[z, :, cut] = new
            if z < PASSES:
                first_planes[z, :, cut] = new
            if z >= PLANES - PASSES:
                last_planes[z - (PLANES - PASSES), :, cut] = new
            change = (new - v)[:ROWS]
            squares = squares + change * change
    total = jnp.sum(squares, axis=(0, 1), keepdims=True)
    moved[...] = jnp.where(iota((8, TILE), 1) == 0, total, 0.0)


def gradient_plane(here, above, flux_z_below, inside):
    lane = iota(here.shape, 1)
    ahead = jnp.where(lane == WIDTH - 1, 0.0, pltpu.roll(here, WIDTH - 1, 1))
    dz = above - here
    dy = pltpu.roll(here, EXT - 1, 0) - here
    dx = ahead - here
    scale = lax.rsqrt(dz * dz + dy * dy + dx * dx + EPS_TV)
    scale = jnp.where(inside, scale, 0.0)
    qz, qy, qx = dz * scale, dy * scale, dx * scale
    gradient = flux_z_below - (qz + qy + qx)
    gradient = gradient + pltpu.roll(qy, 1, 0)
    gradient = gradient + jnp.where(lane == 0, 0.0, pltpu.roll(qx, 1, 1))
    return jnp.where(inside, gradient, 0.0), qz


def flux_below(below, here, inside):
    lane = iota(here.shape, 1)
    ahead = jnp.where(lane == WIDTH - 1, 0.0, pltpu.roll(below, WIDTH - 1, 1))
    dz = here - below
    dy = pltpu.roll(below, EXT - 1, 0) - below
    dx = ahead - below
    scale = lax.rsqrt(dz * dz + dy * dy + dx * dx + EPS_TV)
    return jnp.where(inside, dz * scale, 0.0)


def gradients(f, margin):
    slab, slabs = lax.axis_index("gz"), lax.axis_size("gz")
    rows = inside_rows(lax.axis_index("gy"))
    outside = (len(f) - PLANES) // 2

    def inside(i):
        z = slab * PLANES + i - outside
        return rows & (z >= 0) & (z < slabs * PLANES)

    flux = flux_below(f[margin - 1][...], f[margin][...], inside(margin - 1))
    for i in range(margin, len(f) - margin):
        g, flux = gradient_plane(f[i][...], f[i + 1][...], flux, inside(i))
        yield i, g


def planes_of(*refs):
    return [ref.at[i] for ref in refs for i in range(ref.shape[0])]


def write_sums(f, moved, parts):
    squares = jnp.zeros((ROWS, WIDTH), F32)
    for _, g in gradients(f, (len(f) - PLANES) // 2):
        squares = squares + g[:ROWS] * g[:ROWS]
    total = jnp.sum(squares, axis=(0, 1), keepdims=True)
    row = moved[:1] + jnp.where(iota((1, TILE), 1) == 1, total, 0.0)
    parts[...] = jnp.broadcast_to(row, parts.shape)


def first_sums_kernel(f, below, above, moved, parts):
    planes = planes_of(below, f, above)
    write_sums(planes, moved, parts)


def step_length(sums):
    row = jnp.sum(sums[...], axis=0, keepdims=True)
    lane = iota(row.shape, 1)
    moved = jnp.sum(jnp.where(lane == 0, row, 0.0), axis=1, keepdims=True)
    total = jnp.sum(jnp.where(lane == 1, row, 0.0), axis=1, keepdims=True)
    return TV_ALPHA * jnp.sqrt(moved) / jnp.sqrt(total + EPS_NORM)


def next_sums_kernel(sums, moved, *refs):
    f, f_out, parts = planes_of(*refs[:-2]), refs[-2], refs[-1]
    step = step_length(sums)
    for i, g in gradients(f, 1):
        f_out[i - 1] = f[i][...] - step * g
    write_sums(planes_of(f_out), moved, parts)


def last_step_kernel(sums, f_in, out):
    f = planes_of(f_in)
    step = step_length(sums)
    for i, g in gradients(f, 1):
        out[i - 1] = (f[i][...] - step * g)[:ROWS]


def call(kernel, shapes, args, scratch=(), flops=0, fetched=0, room=16):
    shapes = [jax.ShapeDtypeStruct(shape, dtype) for shape, dtype in shapes]
    moved = sum(a.size * a.dtype.itemsize for a in list(args) + shapes)
    out = pl.pallas_call(
        kernel,
        out_shape=shapes,
        in_specs=[VMEM] * (len(args) - fetched) + [pl.BlockSpec(memory_space=pltpu.HBM)] * fetched,
        out_specs=[VMEM] * len(shapes),
        scratch_shapes=list(scratch),
        compiler_params=pltpu.CompilerParams(vmem_limit_bytes=room * 1024 * 1024),
        cost_estimate=pl.CostEstimate(flops=flops, bytes_accessed=moved, transcendentals=0),
    )(*args)
    return out


def per_device(
    volume, measured, row_norm, col_norm, ray_weight, tiles, tile_kind, tile_band, band_start
):
    slabs, blocks = lax.axis_size("gz"), lax.axis_size("gy")
    block = lax.axis_index("gy")
    other_chip = [(i, i ^ 2) for i in range(blocks)]
    other_core = [(i, i ^ 1) for i in range(blocks)]
    flat = volume.reshape(PLANES * ROWS, WIDTH)
    weight = jnp.swapaxes(ray_weight, 0, 1)
    kinds, bands = jnp.swapaxes(tile_kind, 0, 1), jnp.swapaxes(tile_band, 0, 1)
    small = jnp.concatenate([(kinds + NK * bands).astype(F32), weight], axis=0)
    lanes = jnp.pad(weight, ((0, PLANES * ROWS - ROWS), (0, TILE - ANGLES)))

    def outgoing(first, tiles_sent):
        columns = lax.dynamic_slice_in_dim(flat, first * TILE, tiles_sent * TILE, axis=1)
        return jnp.concatenate([columns, lanes], axis=1)

    far = lax.ppermute(outgoing(jnp.where(block >= 2, 0, XT - REACH), REACH), "gy", other_chip)
    beside = block ^ 1
    window = beside * 2 + jnp.where(beside >= 2, 2, 0)
    near = lax.ppermute(outgoing(window, WINDOW), "gy", other_core)
    far, near, small = lax.optimization_barrier((far, near, small))
    farnear = lax.ppermute(far, "gy", other_core)
    half = HALO // 2
    to_before = jnp.concatenate([volume[:, :half], col_norm[:, :half]], axis=1)
    to_after = jnp.concatenate([volume[:, ROWS - half :], col_norm[:, ROWS - half :]], axis=1)
    after = lax.ppermute(to_before, "gy", [(i + 1, i) for i in range(blocks - 1)])
    before = lax.ppermute(to_after, "gy", [(i, i + 1) for i in range(blocks - 1)])

    rows = PLANES * ANGLES
    chunk = ANGLES * QUARTER * PLANES
    slab_proj, weights = call(
        project_kernel,
        [((chunk, TILE), F32), ((EXT, ANGLES), F32)],
        (far, farnear, near, small, flat, tiles),
        [
            pltpu.VMEM((PLANES * ROWS, WINDOW * TILE), F32),
            pltpu.VMEM((rows, WINDOW * TILE), F32),
            pltpu.VMEM((2 * rows, SLOTS * TILE), BF16),
            pltpu.VMEM((SLOTS, TILE, 2 * TILE), BF16),
            pltpu.VMEM((QUARTER, rows, TILE), F32),
            pltpu.SemaphoreType.DMA((3,)),
        ],
        fetched=2,
        room=40,
        flops=2 * WINDOW * 2 * rows * SLOTS * TILE * 2 * TILE,
    )
    chunks = slab_proj.reshape(slabs, XT, TILE)
    owner_rows = lax.all_to_all(chunks, "gz", split_axis=0, concat_axis=0, tiled=True)
    residual, band_resid = call(
        residual_kernel,
        [(measured.shape[1:], F32), ((chunk, TILE), BF16)],
        (owner_rows.reshape(chunk, TILE), measured[0], row_norm[0], band_start),
        [pltpu.VMEM((rows, QUARTER * TILE), F32), pltpu.VMEM((chunk, TILE), F32)],
        flops=2 * 4 * rows * rows * QUARTER * TILE,
    )
    chunks = band_resid.reshape(slabs, XT, TILE)
    held = lax.all_to_all(chunks, "gz", split_axis=0, concat_axis=0, tiled=True)
    held, after, before = lax.optimization_barrier((held.reshape(chunk, TILE), after, before))
    held_far = lax.ppermute(held, "gy", other_chip)
    held_near = lax.ppermute(held, "gy", other_core)
    held_farnear = lax.ppermute(held_far, "gy", other_core)

    ends = ((PASSES, EXT, WIDTH), F32)
    f, first, last, moved = call(
        back_kernel,
        [((PLANES, EXT, WIDTH), F32), ends, ends, ((8, TILE), F32)],
        (
            held, held_near, held_far, held_farnear, small, weights,
            jnp.swapaxes(tiles, 1, 2), volume, col_norm, after, before,
        ),
        [
            pltpu.VMEM((chunk, TILE), F32),
            pltpu.VMEM((XT, rows, TILE), BF16),
            pltpu.VMEM((rows, SLOTS * TILE), BF16),
            pltpu.VMEM((SLOTS, TILE, 2 * TILE), BF16),
            pltpu.VMEM(volume.shape, F32),
            pltpu.VMEM(volume.shape, F32),
            pltpu.VMEM(after.shape, F32),
            pltpu.VMEM(before.shape, F32),
            pltpu.SemaphoreType.DMA((6,)),
        ],
        fetched=5,
        room=46,
        flops=2 * XT * rows * SLOTS * TILE * 2 * TILE,
    )
    upward = [(i, i + 1) for i in range(slabs - 1)]
    downward = [(i + 1, i) for i in range(slabs - 1)]
    below, above = lax.ppermute(last, "gz", upward), lax.ppermute(first, "gz", downward)

    def exchanged(parts):
        return lax.all_to_all(parts, ("gz", "gy"), split_axis=0, concat_axis=0, tiled=True)

    partial = ((slabs * blocks, TILE), F32)
    work = 40 * EXT * WIDTH
    (parts,) = call(
        first_sums_kernel, [partial], (f, below, above, moved), flops=work * PLANES
    )
    sums, pieces_of_f = exchanged(parts), (below, f, above)
    planes = PLANES + 2 * PASSES
    for step in range(PASSES - 1):
        planes -= 2
        f, parts = call(
            next_sums_kernel,
            [((planes, EXT, WIDTH), F32), partial],
            (sums, moved, *pieces_of_f),
            flops=work * (planes + PLANES),
        )
        sums, pieces_of_f = exchanged(parts), (f,)
    (smoothed,) = call(
        last_step_kernel, [(volume.shape, F32)], (sums, f), flops=work * PLANES
    )
    return smoothed, residual[None]


def solution(mesh):
    placed = (
        P("gz", "gy", None),
        P("gz", None, "gy"),
        P("gz", None, "gy"),
        P("gz", "gy", None),
        P(None, "gy"),
        P(),
        P(),
        P(),
        P(),
    )
    return jax.shard_map(
        per_device,
        mesh=mesh,
        in_specs=placed,
        out_specs=(P("gz", "gy", None), P("gz", None, "gy")),
        check_vma=False,
    )
```

```python
import jax
import jax.numpy as jnp
from jax import lax
from jax.experimental import pallas as pl
from jax.experimental.pallas import tpu as pltpu
from jax.sharding import PartitionSpec as P

PASSES = 3
EPS_TV = 0.01
EPS_NORM = 1e-06
RELAX = 1.0
TV_ALPHA = 0.2

F32 = jnp.float32
BF16 = jnp.bfloat16
VMEM = pl.BlockSpec(memory_space=pltpu.VMEM)

PLANES, ROWS, HALO, TILE, XT, NK, ANGLES = 4, 16, 8, 128, 16, 16, 64
EXT = ROWS + HALO
WIDTH = XT * TILE
QUARTER = 4
WINDOW = 8
REACH = 10
SLOTS = 8
GROUP = 4
PAIR = 2


def iota(shape, dim):
    return lax.broadcasted_iota(jnp.int32, shape, dim)


def onehot(condition, dtype=F32):
    return jnp.where(condition, 1.0, 0.0).astype(dtype)


def dot(a, b, transposed=False):
    dims = (((1,), (1 if transposed else 0,)), ((), ()))
    return lax.dot_general(a, b, dims, preferred_element_type=F32)


def pieces(value, count):
    out = []
    for _ in range(count):
        part = value.astype(BF16)
        out.append(part)
        value = value - part.astype(F32)
    return out


def spread_lanes(parts, order, first, width):
    rows, held = parts[0].shape
    lanes = len(order) * width
    copy = onehot(iota((held, lanes), 1) % width + first == iota((held, lanes), 0), BF16)
    group = iota((rows, lanes), 1) // width
    total = None
    for index, part in enumerate(parts):
        chosen = group == -1
        for place, which in enumerate(order):
            if which == index:
                chosen = chosen | (group == place)
        term = jnp.where(chosen, dot(part, copy), 0.0)
        total = term if total is None else total + term
    return total.astype(BF16)


def start_fetches(pairs, arrived):
    fetches = [
        pltpu.make_async_copy(there, here, arrived.at[i]) for i, (there, here) in enumerate(pairs)
    ]
    for fetch in fetches:
        fetch.start()
    return fetches


def code_column(code, tile):
    lane = iota(code.shape, 1)
    column = jnp.sum(jnp.where(lane == tile, code, 0.0), axis=1, keepdims=True)
    return jnp.broadcast_to(column.astype(jnp.int32), (code.shape[0], TILE))


def slot_masks(kind):
    return [onehot((kind & (SLOTS - 1)) == k, BF16) for k in range(SLOTS)]


def pick_half(wide, kind):
    return jnp.where(kind >= SLOTS, wide[:, TILE:], wide[:, :TILE])


def project_kernel(
    far, farnear, near, small, own, tiles, out, weights_out,
    own_here, sums, lhs, rhs, wide, acc, arrived,
):
    block = lax.axis_index("gy")
    first = block * 2 + jnp.where(block >= 2, 2, 0)
    span = WINDOW * TILE
    window = pl.ds(pl.multiple_of(first * TILE, TILE), span)
    inner = pl.ds(pl.multiple_of(block % 2 * 2 * TILE, TILE), span)
    fetches = start_fetches(
        (
            (own.at[:, window], own_here),
            (tiles.at[:SLOTS], rhs.at[:, :, :TILE]),
            (tiles.at[SLOTS:], rhs.at[:, :, TILE:]),
        ),
        arrived,
    )
    acc[...] = jnp.zeros_like(acc)
    sources = ((far, 2, inner), (farnear, 3, inner), (near, 1, slice(0, span)), (own_here, 0, slice(0, span)))
    weight = [ref[:ROWS, ref.shape[1] - TILE :][:, :ANGLES] for ref in (far, farnear, near)]
    weight = pieces(jnp.concatenate([*weight, small[XT:]], axis=0).T, 3)
    row = iota((EXT, 1), 0)
    wanted = block * ROWS + row - jnp.where(row >= ROWS + HALO // 2, EXT, 0)
    lane = iota((EXT, ANGLES), 1)
    held_row = jnp.zeros((EXT, ANGLES), jnp.int32)
    for order, (_, flip, _) in enumerate(sources):
        mine = lane // ROWS == order
        held_row = held_row + jnp.where(mine, (block ^ flip) * ROWS + lane % ROWS, 0)
    choose = onehot(held_row == wanted, BF16)
    picked = jnp.zeros((EXT, ANGLES), F32)
    for part in weight:
        picked = picked + dot(choose, part, transposed=True)
    for order, (ref, _, lanes) in enumerate(sources):
        if order == 3:
            fetches[0].wait()
        left = spread_lanes(weight, (0, 0, 1, 1, 0, 2), order * ROWS, ROWS)
        for z in range(PLANES):
            v = pieces(ref[z * ROWS : (z + 1) * ROWS, lanes], 3)
            right = jnp.concatenate([v[0], v[1], v[0], v[1], v[2], v[0]], axis=0)
            rays = dot(left, right).astype(BF16).astype(F32)
            here = sums.at[z * ANGLES : (z + 1) * ANGLES, :]
            here[...] = rays if order == 0 else here[...] + rays
    weights_out[...] = picked
    for fetch in fetches[1:]:
        fetch.wait()
    code = small[:XT].T
    rows = PLANES * ANGLES
    columns = [code_column(code, first + j) for j in range(WINDOW)]

    def build(group):
        for j in range(group * PAIR, (group + 1) * PAIR):
            masks = slot_masks(columns[j] & (NK - 1))
            for z in range(PLANES):
                part = sums[z * ANGLES : (z + 1) * ANGLES, j * TILE : (j + 1) * TILE]
                for p, piece in enumerate(pieces(part, 2)):
                    at = ((j * 2 + p) * PLANES + z) * ANGLES
                    for k in range(SLOTS):
                        lhs[at : at + ANGLES, k * TILE : (k + 1) * TILE] = piece * masks[k]
        part = slice(group * PAIR * 2 * rows, (group + 1) * PAIR * 2 * rows)
        wide[part] = dot(lhs[part], rhs[...].reshape(SLOTS * TILE, 2 * TILE))

    def place(group):
        for j in range(group * PAIR, (group + 1) * PAIR):
            kind, band = columns[j] & (NK - 1), columns[j] >> 4
            for z in range(PLANES):
                at = (j * 2 * PLANES + z) * ANGLES
                tile = pick_half(wide[at : at + ANGLES] + wide[at + rows : at + rows + ANGLES], kind)
                for t in range(QUARTER):
                    here = acc.at[t, z * ANGLES : (z + 1) * ANGLES, :]
                    here[...] += jnp.where(band == block * QUARTER + t, tile, 0.0)

    for group in range(WINDOW // PAIR):
        build(group)
        if group > 0:
            place(group - 1)
    place(WINDOW // PAIR - 1)
    for t in range(QUARTER):
        for z in range(PLANES):
            out[pl.ds(t * PLANES + z, ANGLES, stride=XT), :] = acc[
                t, z * ANGLES : (z + 1) * ANGLES, :
            ]


def residual_kernel(rows_in, measured, norm, starts, resid, band_out, gathered, placed):
    angle = lax.axis_index("gz")
    slabs = starts.shape[1]
    total = PLANES * slabs
    mine = jnp.where(iota(starts.shape, 0) == angle, starts[...], 0).astype(F32)
    first = jnp.sum(mine, axis=0, keepdims=True)
    spread = onehot(iota((slabs, total), 1) % slabs == iota((slabs, total), 0), BF16)
    land = dot(jnp.broadcast_to(first, (8, slabs)).astype(BF16), spread)[:1]
    land = land.astype(jnp.int32) + iota((1, total), 1) // slabs
    place = onehot(iota((total, total), 0) == land, BF16)
    r = iota((total, slabs), 0)
    own = jnp.where(r % slabs == iota((total, slabs), 1), first, 0.0)
    land_col = jnp.sum(own, axis=1, keepdims=True).astype(jnp.int32)
    land_col = land_col + iota((total, 1), 0) // slabs
    take = onehot(iota((total, total), 1) == land_col, BF16)
    for t in range(QUARTER):
        for z in range(PLANES):
            gathered[z * slabs : (z + 1) * slabs, t * TILE : (t + 1) * TILE] = rows_in[
                pl.ds(t * PLANES + z, slabs, stride=XT), :
            ]
    projection = None
    for part in pieces(gathered[...], 3):
        term = dot(place, part)
        projection = term if projection is None else projection + term
    residual = (measured[...] - projection) / norm[...]
    resid[...] = residual
    rows = dot(take, residual.astype(BF16))
    for t in range(QUARTER):
        for z in range(PLANES):
            placed[pl.ds(t * PLANES + z, slabs, stride=XT), :] = rows[
                z * slabs : (z + 1) * slabs, t * TILE : (t + 1) * TILE
            ]
    band_out[...] = placed[...].astype(BF16)


def inside_rows(block):
    row = iota((EXT, 1), 0)
    y = block * ROWS + row - jnp.where(row >= ROWS + HALO // 2, EXT, 0)
    return (y >= 0) & (y < lax.axis_size("gy") * ROWS)


def back_kernel(
    b0, b1, b2, b3, small, weights, tiles, volume, norm, after, before,
    updated, first_planes, last_planes, moved,
    flat, rows_by_tile, lhs, rhs, wide,
    volume_here, norm_here, after_here, before_here, arrived,
):
    block = lax.axis_index("gy")
    fetches = start_fetches(
        (
            (volume, volume_here),
            (norm, norm_here),
            (after, after_here),
            (before, before_here),
        ),
        arrived,
    )
    left = spread_lanes(pieces(weights[...], 2), (0, 0, 1), 0, ANGLES)

    def arrange(flip, ref):
        flat[...] = ref[...].astype(F32)
        for t in range(QUARTER):
            for z in range(PLANES):
                rows_by_tile[(block ^ flip) * QUARTER + t, z * ANGLES : (z + 1) * ANGLES, :] = (
                    flat[pl.ds(t * PLANES + z, ANGLES, stride=XT), :].astype(BF16)
                )

    for flip, ref in enumerate((b0, b1, b2, b3)):
        arrange(flip, ref)
    for k in range(SLOTS):
        rhs[k, :, :TILE] = tiles[k]
        rhs[k, :, TILE:] = tiles[k + SLOTS]
    for fetch in fetches:
        fetch.wait()
    code = small[:XT].T
    inside = inside_rows(block)
    low = iota((HALO, 2 * TILE), 0) < HALO // 2
    squares = jnp.zeros((ROWS, 2 * TILE), F32)
    kinds = []
    rows = PLANES * ANGLES

    def build(group):
        for j in range(group * GROUP, (group + 1) * GROUP):
            column = code_column(code, j)
            kind, band = column & (NK - 1), column >> 4
            kinds.append(kind)
            masks = slot_masks(kind)
            near = [t for t in range(j - 2, j + 3) if 0 <= t < XT]
            at_band = [onehot(band == t, BF16) for t in near]
            for z in range(PLANES):
                here = slice(z * ANGLES, (z + 1) * ANGLES)
                chosen = None
                for t, mask in zip(near, at_band):
                    term = rows_by_tile[t, here, :] * mask
                    chosen = term if chosen is None else chosen + term
                first = (j * PLANES + z) * ANGLES
                for k in range(SLOTS):
                    lhs[first : first + ANGLES, k * TILE : (k + 1) * TILE] = chosen * masks[k]
        part = slice(group * GROUP * rows, (group + 1) * GROUP * rows)
        wide[part] = dot(lhs[part], rhs[...].reshape(SLOTS * TILE, 2 * TILE))

    def back_tile(j, z):
        first = (j * PLANES + z) * ANGLES
        return pick_half(wide[first : first + ANGLES], kinds[j])

    def finish(group, squares):
        for pair in range(group * GROUP // 2, (group + 1) * GROUP // 2):
            cut = slice(2 * pair * TILE, (2 * pair + 2) * TILE)
            news = []
            for z in range(PLANES):
                back = jnp.concatenate([back_tile(2 * pair, z), back_tile(2 * pair + 1, z)], axis=1)
                b = pieces(back, 2)
                smeared = dot(left, jnp.concatenate([b[0], b[1], b[0]], axis=0))
                up, down = after_here[z, :, cut], before_here[z, :, cut]
                v = jnp.concatenate(
                    [volume_here[z, :, cut], jnp.where(low, up, pltpu.roll(down, HALO // 2, 0))], axis=0
                )
                n = jnp.concatenate(
                    [norm_here[z, :, cut], jnp.where(low, pltpu.roll(up, HALO // 2, 0), down)], axis=0
                )
                new = v + RELAX * smeared / jnp.where(inside, n, 1.0)
                updated[z, :, cut] = new
                news.append(new)
                change = (new - v)[:ROWS]
                squares = squares + change * change
            first_planes[:, cut] = packed_end(news)
            last_planes[:, cut] = packed_end(news[::-1])
        return squares

    for group in range(XT // GROUP):
        build(group)
        if group > 0:
            squares = finish(group - 1, squares)
    squares = finish(XT // GROUP - 1, squares)
    total = jnp.sum(squares, axis=(0, 1), keepdims=True)
    moved[...] = jnp.where(iota((8, TILE), 1) == 0, total, 0.0)


def packed_end(planes):
    near, *others = planes[:PASSES]
    sent = pieces(near, 2)
    held = sent[0].astype(F32) + sent[1].astype(F32)
    for plane in others:
        sent.append((plane - held).astype(BF16))
        held = held + sent[-1].astype(F32)
    return jnp.concatenate([part.astype(F32) for part in sent], axis=0).astype(BF16)


def unpack_end(ref, planes):
    sent = ref[...].astype(F32)
    held = sent[:EXT]
    for i, plane in enumerate(planes):
        held = held + sent[(i + 1) * EXT : (i + 2) * EXT]
        plane[...] = held


def gradient_plane(here, above, flux_z_below, inside):
    lane = iota(here.shape, 1)
    ahead = jnp.where(lane == WIDTH - 1, 0.0, pltpu.roll(here, WIDTH - 1, 1))
    dz = above - here
    dy = pltpu.roll(here, EXT - 1, 0) - here
    dx = ahead - here
    scale = lax.rsqrt(dz * dz + dy * dy + dx * dx + EPS_TV)
    scale = jnp.where(inside, scale, 0.0)
    qz, qy, qx = dz * scale, dy * scale, dx * scale
    gradient = flux_z_below - (qz + qy + qx)
    gradient = gradient + pltpu.roll(qy, 1, 0)
    gradient = gradient + jnp.where(lane == 0, 0.0, pltpu.roll(qx, 1, 1))
    return jnp.where(inside, gradient, 0.0), qz


def flux_below(below, here, inside):
    lane = iota(here.shape, 1)
    ahead = jnp.where(lane == WIDTH - 1, 0.0, pltpu.roll(below, WIDTH - 1, 1))
    dz = here - below
    dy = pltpu.roll(below, EXT - 1, 0) - below
    dx = ahead - below
    scale = lax.rsqrt(dz * dz + dy * dy + dx * dx + EPS_TV)
    return jnp.where(inside, dz * scale, 0.0)


def gradients(f, first, last):
    slab, slabs = lax.axis_index("gz"), lax.axis_size("gz")
    rows = inside_rows(lax.axis_index("gy"))
    outside = (len(f) - PLANES) // 2

    def inside(i):
        z = slab * PLANES + i - outside
        return rows & (z >= 0) & (z < slabs * PLANES)

    flux = flux_below(f[first - 1](), f[first](), inside(first - 1))
    for i in range(first, last):
        g, flux = gradient_plane(f[i](), f[i + 1](), flux, inside(i))
        yield i, g


def loaders(ref):
    return [lambda i=i: ref[i] for i in range(ref.shape[0])]


def write_sums(f, moved, g_out, parts):
    outside = (len(f) - PLANES) // 2
    squares = jnp.zeros((ROWS, WIDTH), F32)
    for i, g in gradients(f, outside, outside + PLANES):
        g_out[i - outside] = g
        squares = squares + g[:ROWS] * g[:ROWS]
    total = jnp.sum(squares, axis=(0, 1), keepdims=True)
    row = moved[:1] + jnp.where(iota((1, TILE), 1) == 1, total, 0.0)
    parts[...] = jnp.broadcast_to(row, parts.shape)


def with_ends(f, below, above, low, high):
    count = low.shape[0]
    unpack_end(below, [low.at[count - 1 - i] for i in range(count)])
    unpack_end(above, [high.at[i] for i in range(count)])
    return [*loaders(low), *loaders(f), *loaders(high)]


def first_sums_kernel(f, below, above, moved, g_out, parts, low, high):
    write_sums(with_ends(f, below, above, low, high), moved, g_out, parts)


def step_length(sums):
    row = jnp.sum(sums[...], axis=0, keepdims=True)
    lane = iota(row.shape, 1)
    moved = jnp.sum(jnp.where(lane == 0, row, 0.0), axis=1, keepdims=True)
    total = jnp.sum(jnp.where(lane == 1, row, 0.0), axis=1, keepdims=True)
    return TV_ALPHA * jnp.sqrt(moved) / jnp.sqrt(total + EPS_NORM)


def next_sums(sums, f, g, moved, f_out, g_out, parts):
    step = step_length(sums)
    outside = (len(f) - PLANES) // 2
    for z in range(PLANES):
        f_out[outside - 1 + z] = f[outside + z]() - step * g[z]
    for first, last in ((1, outside), (outside + PLANES, len(f) - 1)):
        for i, gradient in gradients(f, first, last):
            f_out[i - 1] = f[i]() - step * gradient
    write_sums(loaders(f_out), moved, g_out, parts)


def second_sums_kernel(sums, moved, f, below, above, g, f_out, g_out, parts, low, high):
    next_sums(sums, with_ends(f, below, above, low, high), g, moved, f_out, g_out, parts)


def third_sums_kernel(sums, moved, f, g, f_out, g_out, parts):
    next_sums(sums, loaders(f), g, moved, f_out, g_out, parts)


def last_step_kernel(sums, f, g, out):
    step = step_length(sums)
    for z in range(PLANES):
        out[z] = f[1 + z, :ROWS] - step * g[z, :ROWS]


def call(kernel, shapes, args, scratch=(), flops=0, fetched=0, room=16):
    shapes = [jax.ShapeDtypeStruct(shape, dtype) for shape, dtype in shapes]
    moved = sum(a.size * a.dtype.itemsize for a in list(args) + shapes)
    out = pl.pallas_call(
        kernel,
        out_shape=shapes,
        in_specs=[VMEM] * (len(args) - fetched) + [pl.BlockSpec(memory_space=pltpu.HBM)] * fetched,
        out_specs=[VMEM] * len(shapes),
        scratch_shapes=list(scratch),
        compiler_params=pltpu.CompilerParams(vmem_limit_bytes=room * 1024 * 1024),
        cost_estimate=pl.CostEstimate(flops=flops, bytes_accessed=moved, transcendentals=0),
    )(*args)
    return out


def per_device(
    volume, measured, row_norm, col_norm, ray_weight, tiles, tile_kind, tile_band, band_start
):
    slabs, blocks = lax.axis_size("gz"), lax.axis_size("gy")
    block = lax.axis_index("gy")
    other_chip = [(i, i ^ 2) for i in range(blocks)]
    other_core = [(i, i ^ 1) for i in range(blocks)]
    flat = volume.reshape(PLANES * ROWS, WIDTH)
    weight = jnp.swapaxes(ray_weight, 0, 1)
    kinds, bands = jnp.swapaxes(tile_kind, 0, 1), jnp.swapaxes(tile_band, 0, 1)
    small = jnp.concatenate([(kinds + NK * bands).astype(F32), weight], axis=0)

    def outgoing(rows_sent, weight_sent, first, tiles_sent):
        columns = lax.dynamic_slice_in_dim(rows_sent, first * TILE, tiles_sent * TILE, axis=1)
        lanes = jnp.pad(weight_sent, ((0, PLANES * ROWS - ROWS), (0, TILE - ANGLES)))
        return jnp.concatenate([columns, lanes], axis=1)

    to_chip = outgoing(flat, weight, jnp.where(block >= 2, 0, XT - REACH), REACH)
    to_chip, flat_later, weight_later = lax.optimization_barrier((to_chip, flat, weight))
    far = lax.ppermute(to_chip, "gy", other_chip)
    beside = block ^ 1
    window = beside * 2 + jnp.where(beside >= 2, 2, 0)
    near = lax.ppermute(outgoing(flat_later, weight_later, window, WINDOW), "gy", other_core)
    far, near, small = lax.optimization_barrier((far, near, small))
    farnear = lax.ppermute(far, "gy", other_core)
    half = HALO // 2
    to_before = jnp.concatenate([volume[:, :half], col_norm[:, :half]], axis=1)
    to_after = jnp.concatenate([volume[:, ROWS - half :], col_norm[:, ROWS - half :]], axis=1)
    after = lax.ppermute(to_before, "gy", [(i + 1, i) for i in range(blocks - 1)])
    before = lax.ppermute(to_after, "gy", [(i, i + 1) for i in range(blocks - 1)])

    rows = PLANES * ANGLES
    chunk = ANGLES * QUARTER * PLANES
    slab_proj, weights = call(
        project_kernel,
        [((chunk, TILE), F32), ((EXT, ANGLES), F32)],
        (far, farnear, near, small, flat, tiles),
        [
            pltpu.VMEM((PLANES * ROWS, WINDOW * TILE), F32),
            pltpu.VMEM((rows, WINDOW * TILE), F32),
            pltpu.VMEM((WINDOW * 2 * rows, SLOTS * TILE), BF16),
            pltpu.VMEM((SLOTS, TILE, 2 * TILE), BF16),
            pltpu.VMEM((WINDOW * 2 * rows, 2 * TILE), F32),
            pltpu.VMEM((QUARTER, rows, TILE), F32),
            pltpu.SemaphoreType.DMA((3,)),
        ],
        fetched=2,
        room=40,
        flops=2 * WINDOW * 2 * rows * SLOTS * TILE * 2 * TILE,
    )
    chunks = slab_proj.reshape(slabs, XT, TILE)
    owner_rows = lax.all_to_all(chunks, "gz", split_axis=0, concat_axis=0, tiled=True)
    owner_rows, after, before = lax.optimization_barrier((owner_rows, after, before))
    residual, band_resid = call(
        residual_kernel,
        [(measured.shape[1:], F32), ((chunk, TILE), BF16)],
        (owner_rows.reshape(chunk, TILE), measured[0], row_norm[0], band_start),
        [pltpu.VMEM((rows, QUARTER * TILE), F32), pltpu.VMEM((chunk, TILE), F32)],
        flops=2 * 4 * rows * rows * QUARTER * TILE,
    )
    chunks = band_resid.reshape(slabs, XT, TILE)
    held = lax.all_to_all(chunks, "gz", split_axis=0, concat_axis=0, tiled=True)
    held = held.reshape(chunk, TILE)
    held_far = lax.ppermute(held, "gy", other_chip)
    held_near = lax.ppermute(held, "gy", other_core)
    held_farnear = lax.ppermute(held_far, "gy", other_core)

    ends = (((PASSES + 1) * EXT, WIDTH), BF16)
    f, first, last, moved = call(
        back_kernel,
        [((PLANES, EXT, WIDTH), F32), ends, ends, ((8, TILE), F32)],
        (
            held, held_near, held_far, held_farnear, small, weights,
            jnp.swapaxes(tiles, 1, 2), volume, col_norm, after, before,
        ),
        [
            pltpu.VMEM((chunk, TILE), F32),
            pltpu.VMEM((XT, rows, TILE), BF16),
            pltpu.VMEM((XT * rows, SLOTS * TILE), BF16),
            pltpu.VMEM((SLOTS, TILE, 2 * TILE), BF16),
            pltpu.VMEM((XT * rows, 2 * TILE), F32),
            pltpu.VMEM(volume.shape, F32),
            pltpu.VMEM(volume.shape, F32),
            pltpu.VMEM(after.shape, F32),
            pltpu.VMEM(before.shape, F32),
            pltpu.SemaphoreType.DMA((6,)),
        ],
        fetched=4,
        room=46,
        flops=2 * XT * rows * SLOTS * TILE * 2 * TILE,
    )
    upward = [(i, i + 1) for i in range(slabs - 1)]
    downward = [(i + 1, i) for i in range(slabs - 1)]
    below, above = lax.ppermute(last, "gz", upward), lax.ppermute(first, "gz", downward)

    def exchanged(parts):
        return lax.all_to_all(parts, ("gz", "gy"), split_axis=0, concat_axis=0, tiled=True)

    partial = ((slabs * blocks, TILE), F32)
    block_ext = ((PLANES, EXT, WIDTH), F32)
    work = 40 * EXT * WIDTH
    g, parts = call(
        first_sums_kernel,
        [block_ext, partial],
        (f, below, above, moved),
        [pltpu.VMEM((1, EXT, WIDTH), F32), pltpu.VMEM((1, EXT, WIDTH), F32)],
        flops=work * PLANES,
    )
    f, g, parts = call(
        second_sums_kernel,
        [((PLANES + 4, EXT, WIDTH), F32), block_ext, partial],
        (exchanged(parts), moved, f, below, above, g),
        [pltpu.VMEM((PASSES, EXT, WIDTH), F32), pltpu.VMEM((PASSES, EXT, WIDTH), F32)],
        flops=work * (2 * PLANES + 4),
    )
    f, g, parts = call(
        third_sums_kernel,
        [((PLANES + 2, EXT, WIDTH), F32), block_ext, partial],
        (exchanged(parts), moved, f, g),
        flops=work * (2 * PLANES + 2),
    )
    (smoothed,) = call(
        last_step_kernel, [(volume.shape, F32)], (exchanged(parts), f, g), flops=2 * volume.size
    )
    return smoothed, residual[None]


def solution(mesh):
    placed = (
        P("gz", "gy", None),
        P("gz", None, "gy"),
        P("gz", None, "gy"),
        P("gz", "gy", None),
        P(None, "gy"),
        P(),
        P(),
        P(),
        P(),
    )
    return jax.shard_map(
        per_device,
        mesh=mesh,
        in_specs=placed,
        out_specs=(P("gz", "gy", None), P("gz", None, "gy")),
        check_vma=False,
    )
```

```python
import jax
import jax.numpy as jnp
from jax import lax
from jax.experimental import pallas as pl
from jax.experimental.pallas import tpu as pltpu
from jax.sharding import PartitionSpec as P

PASSES = 3
EPS_TV = 0.01
EPS_NORM = 1e-06
RELAX = 1.0
TV_ALPHA = 0.2

F32 = jnp.float32
BF16 = jnp.bfloat16
VMEM = pl.BlockSpec(memory_space=pltpu.VMEM)

PLANES, ROWS, HALO, TILE, XT, NK, ANGLES = 4, 16, 8, 128, 16, 16, 64
EXT = ROWS + HALO
WIDTH = XT * TILE
QUARTER = 4
WINDOW = 8
REACH = 10
SLOTS = 8
CHIP_ROW = 4
GROUP = 4
PAIR = 2


def iota(shape, dim):
    return lax.broadcasted_iota(jnp.int32, shape, dim)


def onehot(condition, dtype=F32):
    return jnp.where(condition, 1.0, 0.0).astype(dtype)


def dot(a, b, transposed=False):
    dims = (((1,), (1 if transposed else 0,)), ((), ()))
    return lax.dot_general(a, b, dims, preferred_element_type=F32)


def pieces(value, count):
    out = []
    for _ in range(count):
        part = value.astype(BF16)
        out.append(part)
        value = value - part.astype(F32)
    return out


def spread_lanes(parts, order, first, width):
    rows, held = parts[0].shape
    lanes = len(order) * width
    copy = onehot(iota((held, lanes), 1) % width + first == iota((held, lanes), 0), BF16)
    group = iota((rows, lanes), 1) // width
    total = None
    for index, part in enumerate(parts):
        chosen = group == -1
        for place, which in enumerate(order):
            if which == index:
                chosen = chosen | (group == place)
        term = jnp.where(chosen, dot(part, copy), 0.0)
        total = term if total is None else total + term
    return total.astype(BF16)


def start_fetches(pairs, arrived):
    fetches = [
        pltpu.make_async_copy(there, here, arrived.at[i]) for i, (there, here) in enumerate(pairs)
    ]
    for fetch in fetches:
        fetch.start()
    return fetches


def code_column(code, tile):
    lane = iota(code.shape, 1)
    column = jnp.sum(jnp.where(lane == tile, code, 0.0), axis=1, keepdims=True)
    return jnp.broadcast_to(column.astype(jnp.int32), (code.shape[0], TILE))


def slot_masks(kind):
    return [onehot((kind & (SLOTS - 1)) == k, BF16) for k in range(SLOTS)]


def pick_half(wide, kind):
    return jnp.where(kind >= SLOTS, wide[:, TILE:], wide[:, :TILE])


def project_kernel(
    far, farnear, near, small, own, tiles, out, weights_out,
    own_here, sums, lhs, rhs, wide, acc, arrived,
):
    block = lax.axis_index("gy")
    first = block * 2 + jnp.where(block >= 2, 2, 0)
    span = WINDOW * TILE
    window = pl.ds(pl.multiple_of(first * TILE, TILE), span)
    inner = pl.ds(pl.multiple_of(block % 2 * 2 * TILE, TILE), span)
    fetches = start_fetches(
        (
            (own.at[:, window], own_here),
            (tiles.at[:SLOTS], rhs.at[:, :, :TILE]),
            (tiles.at[SLOTS:], rhs.at[:, :, TILE:]),
        ),
        arrived,
    )
    acc[...] = jnp.zeros_like(acc)
    sources = ((far, 2, inner), (farnear, 3, inner), (near, 1, slice(0, span)), (own_here, 0, slice(0, span)))
    weight = [ref[:ROWS, ref.shape[1] - TILE :][:, :ANGLES] for ref in (far, farnear, near)]
    weight = pieces(jnp.concatenate([*weight, small[XT:]], axis=0).T, 3)
    row = iota((EXT, 1), 0)
    wanted = block * ROWS + row - jnp.where(row >= ROWS + HALO // 2, EXT, 0)
    lane = iota((EXT, ANGLES), 1)
    held_row = jnp.zeros((EXT, ANGLES), jnp.int32)
    for order, (_, flip, _) in enumerate(sources):
        mine = lane // ROWS == order
        held_row = held_row + jnp.where(mine, (block ^ flip) * ROWS + lane % ROWS, 0)
    choose = onehot(held_row == wanted, BF16)
    picked = jnp.zeros((EXT, ANGLES), F32)
    for part in weight:
        picked = picked + dot(choose, part, transposed=True)
    for order, (ref, _, lanes) in enumerate(sources):
        if order == 3:
            fetches[0].wait()
        left = spread_lanes(weight, (0, 0, 1, 1, 0, 2), order * ROWS, ROWS)
        for z in range(PLANES):
            v = pieces(ref[z * ROWS : (z + 1) * ROWS, lanes], 3)
            right = jnp.concatenate([v[0], v[1], v[0], v[1], v[2], v[0]], axis=0)
            rays = dot(left, right).astype(BF16).astype(F32)
            here = sums.at[z * ANGLES : (z + 1) * ANGLES, :]
            here[...] = rays if order == 0 else here[...] + rays
    weights_out[...] = picked
    for fetch in fetches[1:]:
        fetch.wait()
    code = small[:XT].T
    rows = PLANES * ANGLES
    columns = [code_column(code, first + j) for j in range(WINDOW)]

    def build(group):
        for j in range(group * PAIR, (group + 1) * PAIR):
            masks = slot_masks(columns[j] & (NK - 1))
            for z in range(PLANES):
                part = sums[z * ANGLES : (z + 1) * ANGLES, j * TILE : (j + 1) * TILE]
                for p, piece in enumerate(pieces(part, 2)):
                    at = ((j * 2 + p) * PLANES + z) * ANGLES
                    for k in range(SLOTS):
                        lhs[at : at + ANGLES, k * TILE : (k + 1) * TILE] = piece * masks[k]
        part = slice(group * PAIR * 2 * rows, (group + 1) * PAIR * 2 * rows)
        wide[part] = dot(lhs[part], rhs[...].reshape(SLOTS * TILE, 2 * TILE))

    def place(group):
        for j in range(group * PAIR, (group + 1) * PAIR):
            kind, band = columns[j] & (NK - 1), columns[j] >> 4
            for z in range(PLANES):
                at = (j * 2 * PLANES + z) * ANGLES
                tile = pick_half(wide[at : at + ANGLES] + wide[at + rows : at + rows + ANGLES], kind)
                for t in range(QUARTER):
                    here = acc.at[t, z * ANGLES : (z + 1) * ANGLES, :]
                    here[...] += jnp.where(band == block * QUARTER + t, tile, 0.0)

    for group in range(WINDOW // PAIR):
        build(group)
        if group > 0:
            place(group - 1)
    place(WINDOW // PAIR - 1)
    for t in range(QUARTER):
        for z in range(PLANES):
            out[pl.ds(t * PLANES + z, ANGLES, stride=XT), :] = acc[
                t, z * ANGLES : (z + 1) * ANGLES, :
            ]


def residual_kernel(rows_in, measured, norm, starts, resid, band_out, gathered, placed):
    angle = lax.axis_index("gz")
    slabs = starts.shape[1]
    total = PLANES * slabs
    mine = jnp.where(iota(starts.shape, 0) == angle, starts[...], 0).astype(F32)
    first = jnp.sum(mine, axis=0, keepdims=True)
    spread = onehot(iota((slabs, total), 1) % slabs == iota((slabs, total), 0), BF16)
    land = dot(jnp.broadcast_to(first, (8, slabs)).astype(BF16), spread)[:1]
    land = land.astype(jnp.int32) + iota((1, total), 1) // slabs
    place = onehot(iota((total, total), 0) == land, BF16)
    r = iota((total, slabs), 0)
    own = jnp.where(r % slabs == iota((total, slabs), 1), first, 0.0)
    land_col = jnp.sum(own, axis=1, keepdims=True).astype(jnp.int32)
    land_col = land_col + iota((total, 1), 0) // slabs
    take = onehot(iota((total, total), 1) == land_col, BF16)
    for t in range(QUARTER):
        for z in range(PLANES):
            gathered[z * slabs : (z + 1) * slabs, t * TILE : (t + 1) * TILE] = rows_in[
                pl.ds(t * PLANES + z, slabs, stride=XT), :
            ]
    projection = None
    for part in pieces(gathered[...], 3):
        term = dot(place, part)
        projection = term if projection is None else projection + term
    residual = (measured[...] - projection) / norm[...]
    resid[...] = residual
    rows = dot(take, residual.astype(BF16))
    for t in range(QUARTER):
        for z in range(PLANES):
            placed[pl.ds(t * PLANES + z, slabs, stride=XT), :] = rows[
                z * slabs : (z + 1) * slabs, t * TILE : (t + 1) * TILE
            ]
    band_out[...] = placed[...].astype(BF16)


def inside_rows(block):
    row = iota((EXT, 1), 0)
    y = block * ROWS + row - jnp.where(row >= ROWS + HALO // 2, EXT, 0)
    return (y >= 0) & (y < lax.axis_size("gy") * ROWS)


def back_kernel(
    b0, b1, b2, b3, small, weights, tiles, volume, norm, after, before,
    updated, first_planes, last_planes, far_planes, moved,
    flat, rows_by_tile, lhs, rhs, wide,
    volume_here, norm_here, after_here, before_here, arrived,
):
    block = lax.axis_index("gy")
    fetches = start_fetches(
        (
            (volume, volume_here),
            (norm, norm_here),
            (after, after_here),
            (before, before_here),
        ),
        arrived,
    )
    left = spread_lanes(pieces(weights[...], 2), (0, 0, 1), 0, ANGLES)

    def arrange(flip, ref):
        flat[...] = ref[...].astype(F32)
        for t in range(QUARTER):
            for z in range(PLANES):
                rows_by_tile[(block ^ flip) * QUARTER + t, z * ANGLES : (z + 1) * ANGLES, :] = (
                    flat[pl.ds(t * PLANES + z, ANGLES, stride=XT), :].astype(BF16)
                )

    for flip, ref in enumerate((b0, b1, b2, b3)):
        arrange(flip, ref)
    for k in range(SLOTS):
        rhs[k, :, :TILE] = tiles[k]
        rhs[k, :, TILE:] = tiles[k + SLOTS]
    for fetch in fetches:
        fetch.wait()
    code = small[:XT].T
    inside = inside_rows(block)
    low = iota((HALO, 2 * TILE), 0) < HALO // 2
    squares = jnp.zeros((ROWS, 2 * TILE), F32)
    starts_row = lax.axis_index("gz") % CHIP_ROW == 0
    kinds = []
    rows = PLANES * ANGLES

    def build(group):
        for j in range(group * GROUP, (group + 1) * GROUP):
            column = code_column(code, j)
            kind, band = column & (NK - 1), column >> 4
            kinds.append(kind)
            masks = slot_masks(kind)
            near = [t for t in range(j - 2, j + 3) if 0 <= t < XT]
            at_band = [onehot(band == t, BF16) for t in near]
            for z in range(PLANES):
                here = slice(z * ANGLES, (z + 1) * ANGLES)
                chosen = None
                for t, mask in zip(near, at_band):
                    term = rows_by_tile[t, here, :] * mask
                    chosen = term if chosen is None else chosen + term
                first = (j * PLANES + z) * ANGLES
                for k in range(SLOTS):
                    lhs[first : first + ANGLES, k * TILE : (k + 1) * TILE] = chosen * masks[k]
        part = slice(group * GROUP * rows, (group + 1) * GROUP * rows)
        wide[part] = dot(lhs[part], rhs[...].reshape(SLOTS * TILE, 2 * TILE))

    def back_tile(j, z):
        first = (j * PLANES + z) * ANGLES
        return pick_half(wide[first : first + ANGLES], kinds[j])

    def finish(group, squares):
        for pair in range(group * GROUP // 2, (group + 1) * GROUP // 2):
            cut = slice(2 * pair * TILE, (2 * pair + 2) * TILE)
            news = []
            for z in range(PLANES):
                back = jnp.concatenate([back_tile(2 * pair, z), back_tile(2 * pair + 1, z)], axis=1)
                b = pieces(back, 2)
                smeared = dot(left, jnp.concatenate([b[0], b[1], b[0]], axis=0))
                up, down = after_here[z, :, cut], before_here[z, :, cut]
                v = jnp.concatenate(
                    [volume_here[z, :, cut], jnp.where(low, up, pltpu.roll(down, HALO // 2, 0))], axis=0
                )
                n = jnp.concatenate(
                    [norm_here[z, :, cut], jnp.where(low, pltpu.roll(up, HALO // 2, 0), down)], axis=0
                )
                new = v + RELAX * smeared / jnp.where(inside, n, 1.0)
                updated[z, :, cut] = new
                news.append(new)
                change = (new - v)[:ROWS]
                squares = squares + change * change
            lower, upper = packed_end(news), packed_end(news[::-1])
            first_planes[:, cut] = lower.astype(BF16)
            last_planes[:, cut] = upper.astype(BF16)
            far_planes[:, cut] = jnp.where(starts_row, lower, upper).astype(BF16)
        return squares

    for group in range(XT // GROUP):
        build(group)
        if group > 0:
            squares = finish(group - 1, squares)
    squares = finish(XT // GROUP - 1, squares)
    total = jnp.sum(squares, axis=(0, 1), keepdims=True)
    moved[...] = jnp.where(iota((8, TILE), 1) == 0, total, 0.0)


def packed_end(planes):
    near, *others = planes[:PASSES]
    sent = pieces(near, 2)
    held = sent[0].astype(F32) + sent[1].astype(F32)
    for plane in others:
        sent.append((plane - held).astype(BF16))
        held = held + sent[-1].astype(F32)
    return jnp.concatenate([part.astype(F32) for part in sent], axis=0)


def unpack_end(ref, far, from_far, planes):
    rows = (len(planes) + 1) * EXT
    sent = jnp.where(from_far, far[...].astype(F32)[:rows], ref[...].astype(F32)[:rows])
    held = sent[:EXT]
    for i, plane in enumerate(planes):
        held = held + sent[(i + 1) * EXT : (i + 2) * EXT]
        plane[...] = held


def gradient_plane(here, above, flux_z_below, inside):
    lane = iota(here.shape, 1)
    ahead = jnp.where(lane == WIDTH - 1, 0.0, pltpu.roll(here, WIDTH - 1, 1))
    dz = above - here
    dy = pltpu.roll(here, EXT - 1, 0) - here
    dx = ahead - here
    scale = lax.rsqrt(dz * dz + dy * dy + dx * dx + EPS_TV)
    scale = jnp.where(inside, scale, 0.0)
    qz, qy, qx = dz * scale, dy * scale, dx * scale
    gradient = flux_z_below - (qz + qy + qx)
    gradient = gradient + pltpu.roll(qy, 1, 0)
    gradient = gradient + jnp.where(lane == 0, 0.0, pltpu.roll(qx, 1, 1))
    return jnp.where(inside, gradient, 0.0), qz


def flux_below(below, here, inside):
    lane = iota(here.shape, 1)
    ahead = jnp.where(lane == WIDTH - 1, 0.0, pltpu.roll(below, WIDTH - 1, 1))
    dz = here - below
    dy = pltpu.roll(below, EXT - 1, 0) - below
    dx = ahead - below
    scale = lax.rsqrt(dz * dz + dy * dy + dx * dx + EPS_TV)
    return jnp.where(inside, dz * scale, 0.0)


def gradients(f, first, last):
    slab, slabs = lax.axis_index("gz"), lax.axis_size("gz")
    rows = inside_rows(lax.axis_index("gy"))
    outside = (len(f) - PLANES) // 2

    def inside(i):
        z = slab * PLANES + i - outside
        return rows & (z >= 0) & (z < slabs * PLANES)

    flux = flux_below(f[first - 1](), f[first](), inside(first - 1))
    for i in range(first, last):
        g, flux = gradient_plane(f[i](), f[i + 1](), flux, inside(i))
        yield i, g


def loaders(ref):
    return [lambda i=i: ref[i] for i in range(ref.shape[0])]


def write_sums(f, moved, g_out, parts):
    outside = (len(f) - PLANES) // 2
    squares = jnp.zeros((ROWS, WIDTH), F32)
    for i, g in gradients(f, outside, outside + PLANES):
        g_out[i - outside] = g
        squares = squares + g[:ROWS] * g[:ROWS]
    total = jnp.sum(squares, axis=(0, 1), keepdims=True)
    row = moved[:1] + jnp.where(iota((1, TILE), 1) == 1, total, 0.0)
    parts[...] = jnp.broadcast_to(row, parts.shape)


def with_ends(f, below, above, far, low, high):
    count = low.shape[0]
    place = lax.axis_index("gz") % CHIP_ROW
    unpack_end(below, far, place == 0, [low.at[count - 1 - i] for i in range(count)])
    unpack_end(above, far, place == CHIP_ROW - 1, [high.at[i] for i in range(count)])
    return [*loaders(low), *loaders(f), *loaders(high)]


def first_sums_kernel(far, f, below, above, moved, g_out, parts, low, high):
    write_sums(with_ends(f, below, above, far, low, high), moved, g_out, parts)


def step_length(sums):
    row = jnp.sum(sums[...], axis=0, keepdims=True)
    lane = iota(row.shape, 1)
    moved = jnp.sum(jnp.where(lane == 0, row, 0.0), axis=1, keepdims=True)
    total = jnp.sum(jnp.where(lane == 1, row, 0.0), axis=1, keepdims=True)
    return TV_ALPHA * jnp.sqrt(moved) / jnp.sqrt(total + EPS_NORM)


def next_sums(sums, f, g, moved, f_out, g_out, parts):
    step = step_length(sums)
    outside = (len(f) - PLANES) // 2
    for z in range(PLANES):
        f_out[outside - 1 + z] = f[outside + z]() - step * g[z]
    for first, last in ((1, outside), (outside + PLANES, len(f) - 1)):
        for i, gradient in gradients(f, first, last):
            f_out[i - 1] = f[i]() - step * gradient
    write_sums(loaders(f_out), moved, g_out, parts)


def second_sums_kernel(sums, moved, f, below, above, far, g, f_out, g_out, parts, low, high):
    next_sums(sums, with_ends(f, below, above, far, low, high), g, moved, f_out, g_out, parts)


def third_sums_kernel(sums, moved, f, g, f_out, g_out, parts):
    next_sums(sums, loaders(f), g, moved, f_out, g_out, parts)


def last_step_kernel(sums, f, g, out):
    step = step_length(sums)
    for z in range(PLANES):
        out[z] = f[1 + z, :ROWS] - step * g[z, :ROWS]


def call(kernel, shapes, args, scratch=(), flops=0, fetched=0, room=16):
    shapes = [jax.ShapeDtypeStruct(shape, dtype) for shape, dtype in shapes]
    moved = sum(a.size * a.dtype.itemsize for a in list(args) + shapes)
    out = pl.pallas_call(
        kernel,
        out_shape=shapes,
        in_specs=[VMEM] * (len(args) - fetched) + [pl.BlockSpec(memory_space=pltpu.HBM)] * fetched,
        out_specs=[VMEM] * len(shapes),
        scratch_shapes=list(scratch),
        compiler_params=pltpu.CompilerParams(vmem_limit_bytes=room * 1024 * 1024),
        cost_estimate=pl.CostEstimate(flops=flops, bytes_accessed=moved, transcendentals=0),
    )(*args)
    return out


def per_device(
    volume, measured, row_norm, col_norm, ray_weight, tiles, tile_kind, tile_band, band_start
):
    slabs, blocks = lax.axis_size("gz"), lax.axis_size("gy")
    block = lax.axis_index("gy")
    other_chip = [(i, i ^ 2) for i in range(blocks)]
    other_core = [(i, i ^ 1) for i in range(blocks)]
    flat = volume.reshape(PLANES * ROWS, WIDTH)
    weight = jnp.swapaxes(ray_weight, 0, 1)
    kinds, bands = jnp.swapaxes(tile_kind, 0, 1), jnp.swapaxes(tile_band, 0, 1)
    small = jnp.concatenate([(kinds + NK * bands).astype(F32), weight], axis=0)

    def outgoing(columns, weight_sent):
        lanes = jnp.pad(weight_sent, ((0, PLANES * ROWS - ROWS), (0, TILE - ANGLES)))
        return jnp.concatenate([columns, lanes], axis=1)

    reach = REACH * TILE
    to_chip = outgoing(jnp.where(block >= 2, flat[:, :reach], flat[:, WIDTH - reach :]), weight)
    to_chip, flat_later, weight_later = lax.optimization_barrier((to_chip, flat, weight))
    far = lax.ppermute(to_chip, "gy", other_chip)
    beside = block ^ 1
    window = beside * 2 + jnp.where(beside >= 2, 2, 0)
    columns = lax.dynamic_slice_in_dim(flat_later, window * TILE, WINDOW * TILE, axis=1)
    near = lax.ppermute(outgoing(columns, weight_later), "gy", other_core)
    far, near, small = lax.optimization_barrier((far, near, small))
    farnear = lax.ppermute(far, "gy", other_core)
    half = HALO // 2
    to_before = jnp.concatenate([volume[:, :half], col_norm[:, :half]], axis=1)
    to_after = jnp.concatenate([volume[:, ROWS - half :], col_norm[:, ROWS - half :]], axis=1)
    after = lax.ppermute(to_before, "gy", [(i + 1, i) for i in range(blocks - 1)])
    before = lax.ppermute(to_after, "gy", [(i, i + 1) for i in range(blocks - 1)])

    rows = PLANES * ANGLES
    chunk = ANGLES * QUARTER * PLANES
    slab_proj, weights = call(
        project_kernel,
        [((chunk, TILE), F32), ((EXT, ANGLES), F32)],
        (far, farnear, near, small, flat, tiles),
        [
            pltpu.VMEM((PLANES * ROWS, WINDOW * TILE), F32),
            pltpu.VMEM((rows, WINDOW * TILE), F32),
            pltpu.VMEM((WINDOW * 2 * rows, SLOTS * TILE), BF16),
            pltpu.VMEM((SLOTS, TILE, 2 * TILE), BF16),
            pltpu.VMEM((WINDOW * 2 * rows, 2 * TILE), F32),
            pltpu.VMEM((QUARTER, rows, TILE), F32),
            pltpu.SemaphoreType.DMA((3,)),
        ],
        fetched=2,
        room=40,
        flops=2 * WINDOW * 2 * rows * SLOTS * TILE * 2 * TILE,
    )
    chunks = slab_proj.reshape(slabs, XT, TILE)
    owner_rows = lax.all_to_all(chunks, "gz", split_axis=0, concat_axis=0, tiled=True)
    owner_rows, after, before = lax.optimization_barrier((owner_rows, after, before))
    residual, band_resid = call(
        residual_kernel,
        [(measured.shape[1:], F32), ((chunk, TILE), BF16)],
        (owner_rows.reshape(chunk, TILE), measured[0], row_norm[0], band_start),
        [pltpu.VMEM((rows, QUARTER * TILE), F32), pltpu.VMEM((chunk, TILE), F32)],
        flops=2 * 4 * rows * rows * QUARTER * TILE,
    )
    chunks = band_resid.reshape(slabs, XT, TILE)
    held = lax.all_to_all(chunks, "gz", split_axis=0, concat_axis=0, tiled=True)
    held = held.reshape(chunk, TILE)
    held_far = lax.ppermute(held, "gy", other_chip)
    held_near = lax.ppermute(held, "gy", other_core)
    held_farnear = lax.ppermute(held_far, "gy", other_core)

    ends = (((PASSES + 1) * EXT, WIDTH), BF16)
    f, first, last, far_end, moved = call(
        back_kernel,
        [((PLANES, EXT, WIDTH), F32), ends, ends, ends, ((8, TILE), F32)],
        (
            held, held_near, held_far, held_farnear, small, weights,
            jnp.swapaxes(tiles, 1, 2), volume, col_norm, after, before,
        ),
        [
            pltpu.VMEM((chunk, TILE), F32),
            pltpu.VMEM((XT, rows, TILE), BF16),
            pltpu.VMEM((XT * rows, SLOTS * TILE), BF16),
            pltpu.VMEM((SLOTS, TILE, 2 * TILE), BF16),
            pltpu.VMEM((XT * rows, 2 * TILE), F32),
            pltpu.VMEM(volume.shape, F32),
            pltpu.VMEM(volume.shape, F32),
            pltpu.VMEM(after.shape, F32),
            pltpu.VMEM(before.shape, F32),
            pltpu.SemaphoreType.DMA((6,)),
        ],
        fetched=4,
        room=46,
        flops=2 * XT * rows * SLOTS * TILE * 2 * TILE,
    )
    pairs = [(i, i + 1) for i in range(slabs - 1)]
    within = [(i, j) for i, j in pairs if j % CHIP_ROW]
    across = [(i, j) for i, j in pairs if j % CHIP_ROW == 0]
    far_end = lax.ppermute(far_end, "gz", across + [(j, i) for i, j in across])
    below = lax.ppermute(last, "gz", within)
    above = lax.ppermute(first, "gz", [(j, i) for i, j in within])

    def exchanged(parts):
        return lax.all_to_all(parts, ("gz", "gy"), split_axis=0, concat_axis=0, tiled=True)

    partial = ((slabs * blocks, TILE), F32)
    block_ext = ((PLANES, EXT, WIDTH), F32)
    work = 40 * EXT * WIDTH
    g, parts = call(
        first_sums_kernel,
        [block_ext, partial],
        (far_end, f, below, above, moved),
        [pltpu.VMEM((1, EXT, WIDTH), F32), pltpu.VMEM((1, EXT, WIDTH), F32)],
        flops=work * PLANES,
    )
    f, g, parts = call(
        second_sums_kernel,
        [((PLANES + 4, EXT, WIDTH), F32), block_ext, partial],
        (exchanged(parts), moved, f, below, above, far_end, g),
        [pltpu.VMEM((PASSES, EXT, WIDTH), F32), pltpu.VMEM((PASSES, EXT, WIDTH), F32)],
        flops=work * (2 * PLANES + 4),
    )
    f, g, parts = call(
        third_sums_kernel,
        [((PLANES + 2, EXT, WIDTH), F32), block_ext, partial],
        (exchanged(parts), moved, f, g),
        flops=work * (2 * PLANES + 2),
    )
    (smoothed,) = call(
        last_step_kernel, [(volume.shape, F32)], (exchanged(parts), f, g), flops=2 * volume.size
    )
    return smoothed, residual[None]


def solution(mesh):
    placed = (
        P("gz", "gy", None),
        P("gz", None, "gy"),
        P("gz", None, "gy"),
        P("gz", "gy", None),
        P(None, "gy"),
        P(),
        P(),
        P(),
        P(),
    )
    return jax.shard_map(
        per_device,
        mesh=mesh,
        in_specs=placed,
        out_specs=(P("gz", "gy", None), P("gz", None, "gy")),
        check_vma=False,
    )
```

```python
import jax
import jax.numpy as jnp
from jax import lax
from jax.experimental import pallas as pl
from jax.experimental.pallas import tpu as pltpu
from jax.sharding import PartitionSpec as P

PASSES = 3
EPS_TV = 0.01
EPS_NORM = 1e-06
RELAX = 1.0
TV_ALPHA = 0.2

F32 = jnp.float32
BF16 = jnp.bfloat16
VMEM = pl.BlockSpec(memory_space=pltpu.VMEM)

PLANES, ROWS, HALO, TILE, XT, NK, ANGLES = 4, 16, 8, 128, 16, 16, 64
EXT = ROWS + HALO
WIDTH = XT * TILE
QUARTER = 4
WINDOW = 8
REACH = 10
SLOTS = 8
CHIP_ROW = 4
GROUP = 4
PAIR = 2


def iota(shape, dim):
    return lax.broadcasted_iota(jnp.int32, shape, dim)


def onehot(condition, dtype=F32):
    return jnp.where(condition, 1.0, 0.0).astype(dtype)


def dot(a, b, transposed=False):
    dims = (((1,), (1 if transposed else 0,)), ((), ()))
    return lax.dot_general(a, b, dims, preferred_element_type=F32)


def pieces(value, count):
    out = []
    for _ in range(count):
        part = value.astype(BF16)
        out.append(part)
        value = value - part.astype(F32)
    return out


def spread_lanes(parts, order, first, width):
    rows, held = parts[0].shape
    lanes = len(order) * width
    copy = onehot(iota((held, lanes), 1) % width + first == iota((held, lanes), 0), BF16)
    group = iota((rows, lanes), 1) // width
    total = None
    for index, part in enumerate(parts):
        chosen = group == -1
        for place, which in enumerate(order):
            if which == index:
                chosen = chosen | (group == place)
        term = jnp.where(chosen, dot(part, copy), 0.0)
        total = term if total is None else total + term
    return total.astype(BF16)


def start_fetches(pairs, arrived):
    fetches = [
        pltpu.make_async_copy(there, here, arrived.at[i]) for i, (there, here) in enumerate(pairs)
    ]
    for fetch in fetches:
        fetch.start()
    return fetches


def code_column(code, tile):
    lane = iota(code.shape, 1)
    column = jnp.sum(jnp.where(lane == tile, code, 0.0), axis=1, keepdims=True)
    return jnp.broadcast_to(column.astype(jnp.int32), (code.shape[0], TILE))


def slot_masks(kind):
    return [onehot((kind & (SLOTS - 1)) == k, BF16) for k in range(SLOTS)]


def pick_half(wide, kind):
    return jnp.where(kind >= SLOTS, wide[:, TILE:], wide[:, :TILE])


def project_kernel(
    far, farnear, near, small, own, tiles, out, weights_out,
    own_here, sums, lhs, rhs, wide, acc, arrived,
):
    block = lax.axis_index("gy")
    first = block * 2 + jnp.where(block >= 2, 2, 0)
    span = WINDOW * TILE
    window = pl.ds(pl.multiple_of(first * TILE, TILE), span)
    inner = pl.ds(pl.multiple_of(block % 2 * 2 * TILE, TILE), span)
    fetches = start_fetches(
        (
            (own.at[:, window], own_here),
            (tiles.at[:SLOTS], rhs.at[:, :, :TILE]),
            (tiles.at[SLOTS:], rhs.at[:, :, TILE:]),
        ),
        arrived,
    )
    acc[...] = jnp.zeros_like(acc)
    sources = ((far, 2, inner), (farnear, 3, inner), (near, 1, slice(0, span)), (own_here, 0, slice(0, span)))
    weight = [ref[:ROWS, ref.shape[1] - TILE :][:, :ANGLES] for ref in (far, farnear, near)]
    weight = pieces(jnp.concatenate([*weight, small[XT:]], axis=0).T, 3)
    row = iota((EXT, 1), 0)
    wanted = block * ROWS + row - jnp.where(row >= ROWS + HALO // 2, EXT, 0)
    lane = iota((EXT, ANGLES), 1)
    held_row = jnp.zeros((EXT, ANGLES), jnp.int32)
    for order, (_, flip, _) in enumerate(sources):
        mine = lane // ROWS == order
        held_row = held_row + jnp.where(mine, (block ^ flip) * ROWS + lane % ROWS, 0)
    choose = onehot(held_row == wanted, BF16)
    picked = jnp.zeros((EXT, ANGLES), F32)
    for part in weight:
        picked = picked + dot(choose, part, transposed=True)
    for order, (ref, _, lanes) in enumerate(sources):
        if order == 3:
            fetches[0].wait()
        left = spread_lanes(weight, (0, 0, 1, 1, 0, 2), order * ROWS, ROWS)
        for z in range(PLANES):
            v = pieces(ref[z * ROWS : (z + 1) * ROWS, lanes], 3)
            right = jnp.concatenate([v[0], v[1], v[0], v[1], v[2], v[0]], axis=0)
            rays = dot(left, right).astype(BF16).astype(F32)
            here = sums.at[z * ANGLES : (z + 1) * ANGLES, :]
            here[...] = rays if order == 0 else here[...] + rays
    weights_out[...] = picked
    for fetch in fetches[1:]:
        fetch.wait()
    code = small[:XT].T
    rows = PLANES * ANGLES
    columns = [code_column(code, first + j) for j in range(WINDOW)]

    def build(group):
        for j in range(group * PAIR, (group + 1) * PAIR):
            masks = slot_masks(columns[j] & (NK - 1))
            for z in range(PLANES):
                part = sums[z * ANGLES : (z + 1) * ANGLES, j * TILE : (j + 1) * TILE]
                for p, piece in enumerate(pieces(part, 2)):
                    at = ((j * 2 + p) * PLANES + z) * ANGLES
                    for k in range(SLOTS):
                        lhs[at : at + ANGLES, k * TILE : (k + 1) * TILE] = piece * masks[k]
        part = slice(group * PAIR * 2 * rows, (group + 1) * PAIR * 2 * rows)
        wide[part] = dot(lhs[part], rhs[...].reshape(SLOTS * TILE, 2 * TILE))

    def place(group):
        for j in range(group * PAIR, (group + 1) * PAIR):
            kind, band = columns[j] & (NK - 1), columns[j] >> 4
            for z in range(PLANES):
                at = (j * 2 * PLANES + z) * ANGLES
                tile = pick_half(wide[at : at + ANGLES] + wide[at + rows : at + rows + ANGLES], kind)
                for t in range(QUARTER):
                    here = acc.at[t, z * ANGLES : (z + 1) * ANGLES, :]
                    here[...] += jnp.where(band == block * QUARTER + t, tile, 0.0)

    for group in range(WINDOW // PAIR):
        build(group)
        if group > 0:
            place(group - 1)
    place(WINDOW // PAIR - 1)
    for t in range(QUARTER):
        for z in range(PLANES):
            out[pl.ds(t * PLANES + z, ANGLES, stride=XT), :] = acc[
                t, z * ANGLES : (z + 1) * ANGLES, :
            ]


def residual_kernel(rows_in, measured, norm, starts, resid, band_out, gathered, placed):
    angle = lax.axis_index("gz")
    slabs = starts.shape[1]
    total = PLANES * slabs
    mine = jnp.where(iota(starts.shape, 0) == angle, starts[...], 0).astype(F32)
    first = jnp.sum(mine, axis=0, keepdims=True)
    spread = onehot(iota((slabs, total), 1) % slabs == iota((slabs, total), 0), BF16)
    land = dot(jnp.broadcast_to(first, (8, slabs)).astype(BF16), spread)[:1]
    land = land.astype(jnp.int32) + iota((1, total), 1) // slabs
    place = onehot(iota((total, total), 0) == land, BF16)
    r = iota((total, slabs), 0)
    own = jnp.where(r % slabs == iota((total, slabs), 1), first, 0.0)
    land_col = jnp.sum(own, axis=1, keepdims=True).astype(jnp.int32)
    land_col = land_col + iota((total, 1), 0) // slabs
    take = onehot(iota((total, total), 1) == land_col, BF16)
    for t in range(QUARTER):
        for z in range(PLANES):
            gathered[z * slabs : (z + 1) * slabs, t * TILE : (t + 1) * TILE] = rows_in[
                pl.ds(t * PLANES + z, slabs, stride=XT), :
            ]
    projection = None
    for part in pieces(gathered[...], 3):
        term = dot(place, part)
        projection = term if projection is None else projection + term
    residual = (measured[...] - projection) / norm[...]
    resid[...] = residual
    rows = dot(take, residual.astype(BF16))
    for t in range(QUARTER):
        for z in range(PLANES):
            placed[pl.ds(t * PLANES + z, slabs, stride=XT), :] = rows[
                z * slabs : (z + 1) * slabs, t * TILE : (t + 1) * TILE
            ]
    band_out[...] = placed[...].astype(BF16)


def inside_rows(block):
    row = iota((EXT, 1), 0)
    y = block * ROWS + row - jnp.where(row >= ROWS + HALO // 2, EXT, 0)
    return (y >= 0) & (y < lax.axis_size("gy") * ROWS)


def back_kernel(
    b0, b1, b2, b3, small, weights, tiles, volume, norm, after, before,
    updated, first_planes, last_planes, far_planes, moved,
    flat, rows_by_tile, lhs, rhs, wide,
    volume_here, norm_here, after_here, before_here, arrived,
):
    block = lax.axis_index("gy")
    fetches = start_fetches(
        (
            (volume, volume_here),
            (norm, norm_here),
            (after, after_here),
            (before, before_here),
        ),
        arrived,
    )
    left = spread_lanes(pieces(weights[...], 2), (0, 0, 1), 0, ANGLES)

    def arrange(flip, ref):
        flat[...] = ref[...].astype(F32)
        for t in range(QUARTER):
            for z in range(PLANES):
                rows_by_tile[(block ^ flip) * QUARTER + t, z * ANGLES : (z + 1) * ANGLES, :] = (
                    flat[pl.ds(t * PLANES + z, ANGLES, stride=XT), :].astype(BF16)
                )

    for flip, ref in enumerate((b0, b1, b2, b3)):
        arrange(flip, ref)
    for k in range(SLOTS):
        rhs[k, :, :TILE] = tiles[k]
        rhs[k, :, TILE:] = tiles[k + SLOTS]
    for fetch in fetches:
        fetch.wait()
    code = small[:XT].T
    inside = inside_rows(block)
    low = iota((HALO, 2 * TILE), 0) < HALO // 2
    squares = jnp.zeros((ROWS, 2 * TILE), F32)
    starts_row = lax.axis_index("gz") % CHIP_ROW == 0
    kinds = []
    rows = PLANES * ANGLES

    def build(group):
        for j in range(group * GROUP, (group + 1) * GROUP):
            column = code_column(code, j)
            kind, band = column & (NK - 1), column >> 4
            kinds.append(kind)
            masks = slot_masks(kind)
            near = [t for t in range(j - 2, j + 3) if 0 <= t < XT]
            at_band = [band == t for t in near]
            for z in range(PLANES):
                here = slice(z * ANGLES, (z + 1) * ANGLES)
                chosen = None
                for t, mask in zip(near, at_band):
                    term = rows_by_tile[t, here, :]
                    chosen = term if chosen is None else jnp.where(mask, term, chosen)
                first = (j * PLANES + z) * ANGLES
                for k in range(SLOTS):
                    lhs[first : first + ANGLES, k * TILE : (k + 1) * TILE] = chosen * masks[k]
        part = slice(group * GROUP * rows, (group + 1) * GROUP * rows)
        wide[part] = dot(lhs[part], rhs[...].reshape(SLOTS * TILE, 2 * TILE))

    def back_tile(j, z):
        first = (j * PLANES + z) * ANGLES
        return pick_half(wide[first : first + ANGLES], kinds[j])

    def finish(group, squares):
        for pair in range(group * GROUP // 2, (group + 1) * GROUP // 2):
            cut = slice(2 * pair * TILE, (2 * pair + 2) * TILE)
            news = []
            for z in range(PLANES):
                back = jnp.concatenate([back_tile(2 * pair, z), back_tile(2 * pair + 1, z)], axis=1)
                b = pieces(back, 2)
                smeared = dot(left, jnp.concatenate([b[0], b[1], b[0]], axis=0))
                up, down = after_here[z, :, cut], before_here[z, :, cut]
                v = jnp.concatenate(
                    [volume_here[z, :, cut], jnp.where(low, up, pltpu.roll(down, HALO // 2, 0))], axis=0
                )
                n = jnp.concatenate(
                    [norm_here[z, :, cut], jnp.where(low, pltpu.roll(up, HALO // 2, 0), down)], axis=0
                )
                new = v + RELAX * smeared / jnp.where(inside, n, 1.0)
                updated[z, :, cut] = new
                news.append(new)
                change = (new - v)[:ROWS]
                squares = squares + change * change
            lower, upper = packed_end(news, False), packed_end(news[::-1], True)
            first_planes[:, cut] = lower.astype(BF16)
            last_planes[:, cut] = upper.astype(BF16)
            far_planes[:, cut] = jnp.where(starts_row, lower, upper).astype(BF16)
        return squares

    for group in range(XT // GROUP):
        build(group)
        if group > 0:
            squares = finish(group - 1, squares)
    squares = finish(XT // GROUP - 1, squares)
    total = jnp.sum(squares, axis=(0, 1), keepdims=True)
    moved[...] = jnp.where(iota((8, TILE), 1) == 0, total, 0.0)


def shared_rows(last):
    row = iota((HALO, 1), 0)
    return ((row >= 3) & (row < 7), 3) if last else ((row >= 1) & (row < 5), HALO - 3)


def packed_end(planes, last):
    near, *others = planes[:PASSES]
    sent = [part.astype(F32) for part in pieces(near, 2)]
    held = sent[0] + sent[1]
    for plane in others:
        sent.append((plane - held).astype(BF16).astype(F32))
        held = held + sent[-1]
    second, third = sent[2:]
    from_third, shift = shared_rows(last)
    shared = jnp.where(from_third, pltpu.roll(third[ROWS:], shift, 0), second[ROWS:])
    return jnp.concatenate([*sent[:2], second[:ROWS], third[:ROWS], shared], axis=0)


def unpack_end(ref, far, from_far, last, planes):
    sent = jnp.where(from_far, far[...].astype(F32), ref[...].astype(F32))
    second, third, shared = 2 * EXT, 2 * EXT + ROWS, 2 * EXT + 2 * ROWS
    rolled = pltpu.roll(sent[shared:], HALO - shared_rows(last)[1], 0)
    steps = (
        sent[EXT:second],
        jnp.concatenate([sent[second:third], sent[shared:]], axis=0),
        jnp.concatenate([sent[third:shared], rolled], axis=0),
    )
    held = sent[:EXT]
    for step, plane in zip(steps, planes):
        held = held + step
        plane[...] = held


def gradient_plane(here, above, flux_z_below, inside):
    lane = iota(here.shape, 1)
    ahead = jnp.where(lane == WIDTH - 1, 0.0, pltpu.roll(here, WIDTH - 1, 1))
    dz = above - here
    dy = pltpu.roll(here, EXT - 1, 0) - here
    dx = ahead - here
    scale = lax.rsqrt(dz * dz + dy * dy + dx * dx + EPS_TV)
    scale = jnp.where(inside, scale, 0.0)
    qz, qy, qx = dz * scale, dy * scale, dx * scale
    gradient = flux_z_below - (qz + qy + qx)
    gradient = gradient + pltpu.roll(qy, 1, 0)
    gradient = gradient + jnp.where(lane == 0, 0.0, pltpu.roll(qx, 1, 1))
    return jnp.where(inside, gradient, 0.0), qz


def flux_below(below, here, inside):
    lane = iota(here.shape, 1)
    ahead = jnp.where(lane == WIDTH - 1, 0.0, pltpu.roll(below, WIDTH - 1, 1))
    dz = here - below
    dy = pltpu.roll(below, EXT - 1, 0) - below
    dx = ahead - below
    scale = lax.rsqrt(dz * dz + dy * dy + dx * dx + EPS_TV)
    return jnp.where(inside, dz * scale, 0.0)


def gradients(f, first, last):
    slab, slabs = lax.axis_index("gz"), lax.axis_size("gz")
    rows = inside_rows(lax.axis_index("gy"))
    outside = (len(f) - PLANES) // 2

    def inside(i):
        z = slab * PLANES + i - outside
        return rows & (z >= 0) & (z < slabs * PLANES)

    flux = flux_below(f[first - 1](), f[first](), inside(first - 1))
    for i in range(first, last):
        g, flux = gradient_plane(f[i](), f[i + 1](), flux, inside(i))
        yield i, g


def loaders(ref):
    return [lambda i=i: ref[i] for i in range(ref.shape[0])]


def write_sums(f, moved, g_out, parts):
    outside = (len(f) - PLANES) // 2
    squares = jnp.zeros((ROWS, WIDTH), F32)
    for i, g in gradients(f, outside, outside + PLANES):
        g_out[i - outside] = g
        squares = squares + g[:ROWS] * g[:ROWS]
    total = jnp.sum(squares, axis=(0, 1), keepdims=True)
    row = moved[:1] + jnp.where(iota((1, TILE), 1) == 1, total, 0.0)
    parts[...] = jnp.broadcast_to(row, parts.shape)


def with_ends(f, below, above, far, low, high):
    count = low.shape[0]
    place = lax.axis_index("gz") % CHIP_ROW
    unpack_end(below, far, place == 0, True, [low.at[count - 1 - i] for i in range(count)])
    far_above = place == CHIP_ROW - 1
    unpack_end(above, far, far_above, False, [high.at[i] for i in range(count)])
    return [*loaders(low), *loaders(f), *loaders(high)]


def first_sums_kernel(far, f, below, above, moved, g_out, parts, low, high):
    write_sums(with_ends(f, below, above, far, low, high), moved, g_out, parts)


def step_length(sums):
    row = jnp.sum(sums[...], axis=0, keepdims=True)
    lane = iota(row.shape, 1)
    moved = jnp.sum(jnp.where(lane == 0, row, 0.0), axis=1, keepdims=True)
    total = jnp.sum(jnp.where(lane == 1, row, 0.0), axis=1, keepdims=True)
    return TV_ALPHA * jnp.sqrt(moved) / jnp.sqrt(total + EPS_NORM)


def next_sums(sums, f, g, moved, f_out, g_out, parts):
    step = step_length(sums)
    outside = (len(f) - PLANES) // 2
    for z in range(PLANES):
        f_out[outside - 1 + z] = f[outside + z]() - step * g[z]
    for first, last in ((1, outside), (outside + PLANES, len(f) - 1)):
        for i, gradient in gradients(f, first, last):
            f_out[i - 1] = f[i]() - step * gradient
    write_sums(loaders(f_out), moved, g_out, parts)


def second_sums_kernel(sums, moved, f, below, above, far, g, f_out, g_out, parts, low, high):
    next_sums(sums, with_ends(f, below, above, far, low, high), g, moved, f_out, g_out, parts)


def third_sums_kernel(sums, moved, f, g, f_out, g_out, parts):
    next_sums(sums, loaders(f), g, moved, f_out, g_out, parts)


def last_step_kernel(sums, f, g, out):
    step = step_length(sums)
    for z in range(PLANES):
        out[z] = f[1 + z, :ROWS] - step * g[z, :ROWS]


def call(kernel, shapes, args, scratch=(), flops=0, fetched=0, room=16):
    shapes = [jax.ShapeDtypeStruct(shape, dtype) for shape, dtype in shapes]
    moved = sum(a.size * a.dtype.itemsize for a in list(args) + shapes)
    out = pl.pallas_call(
        kernel,
        out_shape=shapes,
        in_specs=[VMEM] * (len(args) - fetched) + [pl.BlockSpec(memory_space=pltpu.HBM)] * fetched,
        out_specs=[VMEM] * len(shapes),
        scratch_shapes=list(scratch),
        compiler_params=pltpu.CompilerParams(vmem_limit_bytes=room * 1024 * 1024),
        cost_estimate=pl.CostEstimate(flops=flops, bytes_accessed=moved, transcendentals=0),
    )(*args)
    return out


def per_device(
    volume, measured, row_norm, col_norm, ray_weight, tiles, tile_kind, tile_band, band_start
):
    slabs, blocks = lax.axis_size("gz"), lax.axis_size("gy")
    block = lax.axis_index("gy")
    other_chip = [(i, i ^ 2) for i in range(blocks)]
    other_core = [(i, i ^ 1) for i in range(blocks)]
    flat = volume.reshape(PLANES * ROWS, WIDTH)
    weight = jnp.swapaxes(ray_weight, 0, 1)
    kinds, bands = jnp.swapaxes(tile_kind, 0, 1), jnp.swapaxes(tile_band, 0, 1)
    small = jnp.concatenate([(kinds + NK * bands).astype(F32), weight], axis=0)

    def outgoing(columns, weight_sent):
        lanes = jnp.pad(weight_sent, ((0, PLANES * ROWS - ROWS), (0, TILE - ANGLES)))
        return jnp.concatenate([columns, lanes], axis=1)

    reach = REACH * TILE
    to_chip = outgoing(jnp.where(block >= 2, flat[:, :reach], flat[:, WIDTH - reach :]), weight)
    to_chip, flat_later, weight_later = lax.optimization_barrier((to_chip, flat, weight))
    far = lax.ppermute(to_chip, "gy", other_chip)
    beside = block ^ 1
    window = beside * 2 + jnp.where(beside >= 2, 2, 0)
    columns = lax.dynamic_slice_in_dim(flat_later, window * TILE, WINDOW * TILE, axis=1)
    near = lax.ppermute(outgoing(columns, weight_later), "gy", other_core)
    far, near, small = lax.optimization_barrier((far, near, small))
    farnear = lax.ppermute(far, "gy", other_core)
    half = HALO // 2
    to_before = jnp.concatenate([volume[:, :half], col_norm[:, :half]], axis=1)
    to_after = jnp.concatenate([volume[:, ROWS - half :], col_norm[:, ROWS - half :]], axis=1)
    after = lax.ppermute(to_before, "gy", [(i + 1, i) for i in range(blocks - 1)])
    before = lax.ppermute(to_after, "gy", [(i, i + 1) for i in range(blocks - 1)])

    rows = PLANES * ANGLES
    chunk = ANGLES * QUARTER * PLANES
    slab_proj, weights = call(
        project_kernel,
        [((chunk, TILE), F32), ((EXT, ANGLES), F32)],
        (far, farnear, near, small, flat, tiles),
        [
            pltpu.VMEM((PLANES * ROWS, WINDOW * TILE), F32),
            pltpu.VMEM((rows, WINDOW * TILE), F32),
            pltpu.VMEM((WINDOW * 2 * rows, SLOTS * TILE), BF16),
            pltpu.VMEM((SLOTS, TILE, 2 * TILE), BF16),
            pltpu.VMEM((WINDOW * 2 * rows, 2 * TILE), F32),
            pltpu.VMEM((QUARTER, rows, TILE), F32),
            pltpu.SemaphoreType.DMA((3,)),
        ],
        fetched=2,
        room=40,
        flops=2 * WINDOW * 2 * rows * SLOTS * TILE * 2 * TILE,
    )
    chunks = slab_proj.reshape(slabs, XT, TILE)
    owner_rows = lax.all_to_all(chunks, "gz", split_axis=0, concat_axis=0, tiled=True)
    owner_rows, after, before = lax.optimization_barrier((owner_rows, after, before))
    residual, band_resid = call(
        residual_kernel,
        [(measured.shape[1:], F32), ((chunk, TILE), BF16)],
        (owner_rows.reshape(chunk, TILE), measured[0], row_norm[0], band_start),
        [pltpu.VMEM((rows, QUARTER * TILE), F32), pltpu.VMEM((chunk, TILE), F32)],
        flops=2 * 4 * rows * rows * QUARTER * TILE,
    )
    chunks = band_resid.reshape(slabs, XT, TILE)
    held = lax.all_to_all(chunks, "gz", split_axis=0, concat_axis=0, tiled=True)
    held = held.reshape(chunk, TILE)
    held_far = lax.ppermute(held, "gy", other_chip)
    held_near = lax.ppermute(held, "gy", other_core)
    held_farnear = lax.ppermute(held_far, "gy", other_core)

    ends = ((2 * (EXT + ROWS) + HALO, WIDTH), BF16)
    f, first, last, far_end, moved = call(
        back_kernel,
        [((PLANES, EXT, WIDTH), F32), ends, ends, ends, ((8, TILE), F32)],
        (
            held, held_near, held_far, held_farnear, small, weights,
            jnp.swapaxes(tiles, 1, 2), volume, col_norm, after, before,
        ),
        [
            pltpu.VMEM((chunk, TILE), F32),
            pltpu.VMEM((XT, rows, TILE), BF16),
            pltpu.VMEM((XT * rows, SLOTS * TILE), BF16),
            pltpu.VMEM((SLOTS, TILE, 2 * TILE), BF16),
            pltpu.VMEM((XT * rows, 2 * TILE), F32),
            pltpu.VMEM(volume.shape, F32),
            pltpu.VMEM(volume.shape, F32),
            pltpu.VMEM(after.shape, F32),
            pltpu.VMEM(before.shape, F32),
            pltpu.SemaphoreType.DMA((6,)),
        ],
        fetched=4,
        room=46,
        flops=2 * XT * rows * SLOTS * TILE * 2 * TILE,
    )
    pairs = [(i, i + 1) for i in range(slabs - 1)]
    within = [(i, j) for i, j in pairs if j % CHIP_ROW]
    across = [(i, j) for i, j in pairs if j % CHIP_ROW == 0]
    far_end = lax.ppermute(far_end, "gz", across + [(j, i) for i, j in across])
    below = lax.ppermute(last, "gz", within)
    above = lax.ppermute(first, "gz", [(j, i) for i, j in within])

    def exchanged(parts):
        return lax.all_to_all(parts, ("gz", "gy"), split_axis=0, concat_axis=0, tiled=True)

    partial = ((slabs * blocks, TILE), F32)
    block_ext = ((PLANES, EXT, WIDTH), F32)
    work = 40 * EXT * WIDTH
    g, parts = call(
        first_sums_kernel,
        [block_ext, partial],
        (far_end, f, below, above, moved),
        [pltpu.VMEM((1, EXT, WIDTH), F32), pltpu.VMEM((1, EXT, WIDTH), F32)],
        flops=work * PLANES,
    )
    f, g, parts = call(
        second_sums_kernel,
        [((PLANES + 4, EXT, WIDTH), F32), block_ext, partial],
        (exchanged(parts), moved, f, below, above, far_end, g),
        [pltpu.VMEM((PASSES, EXT, WIDTH), F32), pltpu.VMEM((PASSES, EXT, WIDTH), F32)],
        flops=work * (2 * PLANES + 4),
    )
    f, g, parts = call(
        third_sums_kernel,
        [((PLANES + 2, EXT, WIDTH), F32), block_ext, partial],
        (exchanged(parts), moved, f, g),
        flops=work * (2 * PLANES + 2),
    )
    (smoothed,) = call(
        last_step_kernel, [(volume.shape, F32)], (exchanged(parts), f, g), flops=2 * volume.size
    )
    return smoothed, residual[None]


def solution(mesh):
    placed = (
        P("gz", "gy", None),
        P("gz", None, "gy"),
        P("gz", None, "gy"),
        P("gz", "gy", None),
        P(None, "gy"),
        P(),
        P(),
        P(),
        P(),
    )
    return jax.shard_map(
        per_device,
        mesh=mesh,
        in_specs=placed,
        out_specs=(P("gz", "gy", None), P("gz", None, "gy")),
        check_vma=False,
    )
```

```python
import jax
import jax.numpy as jnp
from jax import lax
from jax.experimental import pallas as pl
from jax.experimental.pallas import tpu as pltpu
from jax.sharding import PartitionSpec as P

PASSES = 3
EPS_TV = 0.01
EPS_NORM = 1e-06
RELAX = 1.0
TV_ALPHA = 0.2

F32 = jnp.float32
BF16 = jnp.bfloat16
VMEM = pl.BlockSpec(memory_space=pltpu.VMEM)

PLANES, ROWS, HALO, TILE, XT, NK, ANGLES = 4, 16, 8, 128, 16, 16, 64
EXT = ROWS + HALO
WIDTH = XT * TILE
QUARTER = 4
WINDOW = 8
REACH = 10
SLOTS = 8
CHIP_ROW = 4
GROUP = 4
PAIR = 2


def iota(shape, dim):
    return lax.broadcasted_iota(jnp.int32, shape, dim)


def onehot(condition, dtype=F32):
    return jnp.where(condition, 1.0, 0.0).astype(dtype)


def dot(a, b, transposed=False):
    dims = (((1,), (1 if transposed else 0,)), ((), ()))
    return lax.dot_general(a, b, dims, preferred_element_type=F32)


def pieces(value, count):
    out = []
    for _ in range(count):
        part = value.astype(BF16)
        out.append(part)
        value = value - part.astype(F32)
    return out


def spread_lanes(parts, order, first, width):
    rows, held = parts[0].shape
    lanes = len(order) * width
    copy = onehot(iota((held, lanes), 1) % width + first == iota((held, lanes), 0), BF16)
    group = iota((rows, lanes), 1) // width
    total = None
    for index, part in enumerate(parts):
        chosen = group == -1
        for place, which in enumerate(order):
            if which == index:
                chosen = chosen | (group == place)
        term = jnp.where(chosen, dot(part, copy), 0.0)
        total = term if total is None else total + term
    return total.astype(BF16)


def start_fetches(pairs, arrived):
    fetches = [
        pltpu.make_async_copy(there, here, arrived.at[i]) for i, (there, here) in enumerate(pairs)
    ]
    for fetch in fetches:
        fetch.start()
    return fetches


def code_column(code, tile):
    lane = iota(code.shape, 1)
    column = jnp.sum(jnp.where(lane == tile, code, 0.0), axis=1, keepdims=True)
    return jnp.broadcast_to(column.astype(jnp.int32), (code.shape[0], TILE))


def slot_masks(kind):
    return [onehot((kind & (SLOTS - 1)) == k, BF16) for k in range(SLOTS)]


def pick_half(wide, kind):
    return jnp.where(kind >= SLOTS, wide[:, TILE:], wide[:, :TILE])


def project_kernel(
    far, farnear, near, w_far, w_farnear, w_near, small, own, tiles, out, weights_out,
    own_here, sums, lhs, rhs, wide, acc, arrived,
):
    block = lax.axis_index("gy")
    first = block * 2 + jnp.where(block >= 2, 2, 0)
    span = WINDOW * TILE
    window = pl.ds(pl.multiple_of(first * TILE, TILE), span)
    inner = pl.ds(pl.multiple_of(block % 2 * 2 * TILE, TILE), span)
    fetches = start_fetches(
        (
            (own.at[:, window], own_here),
            (tiles.at[:SLOTS], rhs.at[:, :, :TILE]),
            (tiles.at[SLOTS:], rhs.at[:, :, TILE:]),
        ),
        arrived,
    )
    acc[...] = jnp.zeros_like(acc)
    sources = ((far, 2, inner), (farnear, 3, inner), (near, 1, slice(0, span)), (own_here, 0, slice(0, span)))
    weight = [ref[...] for ref in (w_far, w_farnear, w_near)]
    weight = pieces(jnp.concatenate([*weight, small[XT:]], axis=0).T, 3)
    row = iota((EXT, 1), 0)
    wanted = block * ROWS + row - jnp.where(row >= ROWS + HALO // 2, EXT, 0)
    lane = iota((EXT, ANGLES), 1)
    held_row = jnp.zeros((EXT, ANGLES), jnp.int32)
    for order, (_, flip, _) in enumerate(sources):
        mine = lane // ROWS == order
        held_row = held_row + jnp.where(mine, (block ^ flip) * ROWS + lane % ROWS, 0)
    choose = onehot(held_row == wanted, BF16)
    picked = jnp.zeros((EXT, ANGLES), F32)
    for part in weight:
        picked = picked + dot(choose, part, transposed=True)
    for order, (ref, _, lanes) in enumerate(sources):
        if order == 3:
            fetches[0].wait()
        left = spread_lanes(weight, (0, 0, 1, 1, 0, 2), order * ROWS, ROWS)
        for z in range(PLANES):
            v = pieces(ref[z * ROWS : (z + 1) * ROWS, lanes], 3)
            right = jnp.concatenate([v[0], v[1], v[0], v[1], v[2], v[0]], axis=0)
            rays = dot(left, right).astype(BF16).astype(F32)
            here = sums.at[z * ANGLES : (z + 1) * ANGLES, :]
            here[...] = rays if order == 0 else here[...] + rays
    weights_out[...] = picked
    for fetch in fetches[1:]:
        fetch.wait()
    code = small[:XT].T
    rows = PLANES * ANGLES
    columns = [code_column(code, first + j) for j in range(WINDOW)]

    def build(group):
        for j in range(group * PAIR, (group + 1) * PAIR):
            masks = slot_masks(columns[j] & (NK - 1))
            for z in range(PLANES):
                part = sums[z * ANGLES : (z + 1) * ANGLES, j * TILE : (j + 1) * TILE]
                for p, piece in enumerate(pieces(part, 2)):
                    at = ((j * 2 + p) * PLANES + z) * ANGLES
                    for k in range(SLOTS):
                        lhs[at : at + ANGLES, k * TILE : (k + 1) * TILE] = piece * masks[k]
        part = slice(group * PAIR * 2 * rows, (group + 1) * PAIR * 2 * rows)
        wide[part] = dot(lhs[part], rhs[...].reshape(SLOTS * TILE, 2 * TILE))

    def place(group):
        for j in range(group * PAIR, (group + 1) * PAIR):
            kind, band = columns[j] & (NK - 1), columns[j] >> 4
            for z in range(PLANES):
                at = (j * 2 * PLANES + z) * ANGLES
                tile = pick_half(wide[at : at + ANGLES] + wide[at + rows : at + rows + ANGLES], kind)
                for t in range(QUARTER):
                    here = acc.at[t, z * ANGLES : (z + 1) * ANGLES, :]
                    here[...] += jnp.where(band == block * QUARTER + t, tile, 0.0)

    for group in range(WINDOW // PAIR):
        build(group)
        if group > 0:
            place(group - 1)
    place(WINDOW // PAIR - 1)
    for t in range(QUARTER):
        for z in range(PLANES):
            out[pl.ds(t * PLANES + z, ANGLES, stride=XT), :] = acc[
                t, z * ANGLES : (z + 1) * ANGLES, :
            ]


def residual_kernel(rows_in, measured, norm, starts, resid, band_out, gathered, placed):
    angle = lax.axis_index("gz")
    slabs = starts.shape[1]
    total = PLANES * slabs
    mine = jnp.where(iota(starts.shape, 0) == angle, starts[...], 0).astype(F32)
    first = jnp.sum(mine, axis=0, keepdims=True)
    spread = onehot(iota((slabs, total), 1) % slabs == iota((slabs, total), 0), BF16)
    land = dot(jnp.broadcast_to(first, (8, slabs)).astype(BF16), spread)[:1]
    land = land.astype(jnp.int32) + iota((1, total), 1) // slabs
    place = onehot(iota((total, total), 0) == land, BF16)
    r = iota((total, slabs), 0)
    own = jnp.where(r % slabs == iota((total, slabs), 1), first, 0.0)
    land_col = jnp.sum(own, axis=1, keepdims=True).astype(jnp.int32)
    land_col = land_col + iota((total, 1), 0) // slabs
    take = onehot(iota((total, total), 1) == land_col, BF16)
    for t in range(QUARTER):
        for z in range(PLANES):
            gathered[z * slabs : (z + 1) * slabs, t * TILE : (t + 1) * TILE] = rows_in[
                pl.ds(t * PLANES + z, slabs, stride=XT), :
            ]
    projection = None
    for part in pieces(gathered[...], 3):
        term = dot(place, part)
        projection = term if projection is None else projection + term
    residual = (measured[...] - projection) / norm[...]
    resid[...] = residual
    rows = dot(take, residual.astype(BF16))
    for t in range(QUARTER):
        for z in range(PLANES):
            placed[pl.ds(t * PLANES + z, slabs, stride=XT), :] = rows[
                z * slabs : (z + 1) * slabs, t * TILE : (t + 1) * TILE
            ]
    band_out[...] = placed[...].astype(BF16)


def inside_rows(block):
    row = iota((EXT, 1), 0)
    y = block * ROWS + row - jnp.where(row >= ROWS + HALO // 2, EXT, 0)
    return (y >= 0) & (y < lax.axis_size("gy") * ROWS)


def back_kernel(
    b0, b1, b2, b3, small, weights, tiles, volume, norm, after, before,
    updated, first_planes, last_planes, far_planes, moved,
    flat, rows_by_tile, lhs, rhs, wide,
    volume_here, norm_here, after_here, before_here, arrived,
):
    block = lax.axis_index("gy")
    fetches = start_fetches(
        (
            (volume, volume_here),
            (norm, norm_here),
            (after, after_here),
            (before, before_here),
        ),
        arrived,
    )
    left = spread_lanes(pieces(weights[...], 2), (0, 0, 1), 0, ANGLES)

    def arrange(flip, ref):
        flat[...] = ref[...].astype(F32)
        for t in range(QUARTER):
            for z in range(PLANES):
                rows_by_tile[(block ^ flip) * QUARTER + t, z * ANGLES : (z + 1) * ANGLES, :] = (
                    flat[pl.ds(t * PLANES + z, ANGLES, stride=XT), :].astype(BF16)
                )

    for flip, ref in enumerate((b0, b1, b2, b3)):
        arrange(flip, ref)
    for k in range(SLOTS):
        rhs[k, :, :TILE] = tiles[k]
        rhs[k, :, TILE:] = tiles[k + SLOTS]
    for fetch in fetches:
        fetch.wait()
    code = small[:XT].T
    inside = inside_rows(block)
    low = iota((HALO, 2 * TILE), 0) < HALO // 2
    squares = jnp.zeros((ROWS, 2 * TILE), F32)
    starts_row = lax.axis_index("gz") % CHIP_ROW == 0
    kinds = []
    rows = PLANES * ANGLES

    def build(group):
        for j in range(group * GROUP, (group + 1) * GROUP):
            column = code_column(code, j)
            kind, band = column & (NK - 1), column >> 4
            kinds.append(kind)
            masks = slot_masks(kind)
            near = [t for t in range(j - 2, j + 3) if 0 <= t < XT]
            at_band = [band == t for t in near]
            for z in range(PLANES):
                here = slice(z * ANGLES, (z + 1) * ANGLES)
                chosen = None
                for t, mask in zip(near, at_band):
                    term = rows_by_tile[t, here, :]
                    chosen = term if chosen is None else jnp.where(mask, term, chosen)
                first = (j * PLANES + z) * ANGLES
                for k in range(SLOTS):
                    lhs[first : first + ANGLES, k * TILE : (k + 1) * TILE] = chosen * masks[k]
        part = slice(group * GROUP * rows, (group + 1) * GROUP * rows)
        wide[part] = dot(lhs[part], rhs[...].reshape(SLOTS * TILE, 2 * TILE))

    def back_tile(j, z):
        first = (j * PLANES + z) * ANGLES
        return pick_half(wide[first : first + ANGLES], kinds[j])

    def finish(group, squares):
        for pair in range(group * GROUP // 2, (group + 1) * GROUP // 2):
            cut = slice(2 * pair * TILE, (2 * pair + 2) * TILE)
            news = []
            for z in range(PLANES):
                back = jnp.concatenate([back_tile(2 * pair, z), back_tile(2 * pair + 1, z)], axis=1)
                b = pieces(back, 2)
                smeared = dot(left, jnp.concatenate([b[0], b[1], b[0]], axis=0))
                up, down = after_here[z, :, cut], before_here[z, :, cut]
                v = jnp.concatenate(
                    [volume_here[z, :, cut], jnp.where(low, up, pltpu.roll(down, HALO // 2, 0))], axis=0
                )
                n = jnp.concatenate(
                    [norm_here[z, :, cut], jnp.where(low, pltpu.roll(up, HALO // 2, 0), down)], axis=0
                )
                new = v + RELAX * smeared / jnp.where(inside, n, 1.0)
                updated[z, :, cut] = new
                news.append(new)
                change = (new - v)[:ROWS]
                squares = squares + change * change
            lower, upper = packed_end(news, False), packed_end(news[::-1], True)
            first_planes[:, cut] = lower.astype(BF16)
            last_planes[:, cut] = upper.astype(BF16)
            far_planes[:, cut] = jnp.where(starts_row, lower, upper).astype(BF16)
        return squares

    for group in range(XT // GROUP):
        build(group)
        if group > 0:
            squares = finish(group - 1, squares)
    squares = finish(XT // GROUP - 1, squares)
    total = jnp.sum(squares, axis=(0, 1), keepdims=True)
    moved[...] = jnp.where(iota((8, TILE), 1) == 0, total, 0.0)


def shared_rows(last):
    row = iota((HALO, 1), 0)
    return ((row >= 3) & (row < 7), 3) if last else ((row >= 1) & (row < 5), HALO - 3)


def packed_end(planes, last):
    near, *others = planes[:PASSES]
    sent = [part.astype(F32) for part in pieces(near, 2)]
    held = sent[0] + sent[1]
    for plane in others:
        sent.append((plane - held).astype(BF16).astype(F32))
        held = held + sent[-1]
    second, third = sent[2:]
    from_third, shift = shared_rows(last)
    shared = jnp.where(from_third, pltpu.roll(third[ROWS:], shift, 0), second[ROWS:])
    return jnp.concatenate([*sent[:2], second[:ROWS], third[:ROWS], shared], axis=0)


def unpack_end(ref, far, from_far, last, planes):
    sent = jnp.where(from_far, far[...].astype(F32), ref[...].astype(F32))
    second, third, shared = 2 * EXT, 2 * EXT + ROWS, 2 * EXT + 2 * ROWS
    rolled = pltpu.roll(sent[shared:], HALO - shared_rows(last)[1], 0)
    steps = (
        sent[EXT:second],
        jnp.concatenate([sent[second:third], sent[shared:]], axis=0),
        jnp.concatenate([sent[third:shared], rolled], axis=0),
    )
    held = sent[:EXT]
    for step, plane in zip(steps, planes):
        held = held + step
        plane[...] = held


def gradient_plane(here, above, flux_z_below, inside):
    lane = iota(here.shape, 1)
    ahead = jnp.where(lane == WIDTH - 1, 0.0, pltpu.roll(here, WIDTH - 1, 1))
    dz = above - here
    dy = pltpu.roll(here, EXT - 1, 0) - here
    dx = ahead - here
    scale = lax.rsqrt(dz * dz + dy * dy + dx * dx + EPS_TV)
    scale = jnp.where(inside, scale, 0.0)
    qz, qy, qx = dz * scale, dy * scale, dx * scale
    gradient = flux_z_below - (qz + qy + qx)
    gradient = gradient + pltpu.roll(qy, 1, 0)
    gradient = gradient + jnp.where(lane == 0, 0.0, pltpu.roll(qx, 1, 1))
    return jnp.where(inside, gradient, 0.0), qz


def flux_below(below, here, inside):
    lane = iota(here.shape, 1)
    ahead = jnp.where(lane == WIDTH - 1, 0.0, pltpu.roll(below, WIDTH - 1, 1))
    dz = here - below
    dy = pltpu.roll(below, EXT - 1, 0) - below
    dx = ahead - below
    scale = lax.rsqrt(dz * dz + dy * dy + dx * dx + EPS_TV)
    return jnp.where(inside, dz * scale, 0.0)


def gradients(f, first, last):
    slab, slabs = lax.axis_index("gz"), lax.axis_size("gz")
    rows = inside_rows(lax.axis_index("gy"))
    outside = (len(f) - PLANES) // 2

    def inside(i):
        z = slab * PLANES + i - outside
        return rows & (z >= 0) & (z < slabs * PLANES)

    flux = flux_below(f[first - 1](), f[first](), inside(first - 1))
    for i in range(first, last):
        g, flux = gradient_plane(f[i](), f[i + 1](), flux, inside(i))
        yield i, g


def loaders(ref):
    return [lambda i=i: ref[i] for i in range(ref.shape[0])]


def write_sums(f, moved, g_out, parts):
    outside = (len(f) - PLANES) // 2
    squares = jnp.zeros((ROWS, WIDTH), F32)
    for i, g in gradients(f, outside, outside + PLANES):
        g_out[i - outside] = g
        squares = squares + g[:ROWS] * g[:ROWS]
    total = jnp.sum(squares, axis=(0, 1), keepdims=True)
    row = moved[:1] + jnp.where(iota((1, TILE), 1) == 1, total, 0.0)
    parts[...] = jnp.broadcast_to(row, parts.shape)


def with_ends(f, below, above, far, low, high):
    count = low.shape[0]
    place = lax.axis_index("gz") % CHIP_ROW
    unpack_end(below, far, place == 0, True, [low.at[count - 1 - i] for i in range(count)])
    far_above = place == CHIP_ROW - 1
    unpack_end(above, far, far_above, False, [high.at[i] for i in range(count)])
    return [*loaders(low), *loaders(f), *loaders(high)]


def first_sums_kernel(far, f, below, above, moved, g_out, parts, low, high):
    write_sums(with_ends(f, below, above, far, low, high), moved, g_out, parts)


def step_length(sums):
    row = jnp.sum(sums[...], axis=0, keepdims=True)
    lane = iota(row.shape, 1)
    moved = jnp.sum(jnp.where(lane == 0, row, 0.0), axis=1, keepdims=True)
    total = jnp.sum(jnp.where(lane == 1, row, 0.0), axis=1, keepdims=True)
    return TV_ALPHA * jnp.sqrt(moved) / jnp.sqrt(total + EPS_NORM)


def next_sums(sums, f, g, moved, f_out, g_out, parts):
    step = step_length(sums)
    outside = (len(f) - PLANES) // 2
    for z in range(PLANES):
        f_out[outside - 1 + z] = f[outside + z]() - step * g[z]
    for first, last in ((1, outside), (outside + PLANES, len(f) - 1)):
        for i, gradient in gradients(f, first, last):
            f_out[i - 1] = f[i]() - step * gradient
    write_sums(loaders(f_out), moved, g_out, parts)


def second_sums_kernel(sums, moved, f, below, above, far, g, f_out, g_out, parts, low, high):
    next_sums(sums, with_ends(f, below, above, far, low, high), g, moved, f_out, g_out, parts)


def third_sums_kernel(sums, moved, f, g, f_out, g_out, parts):
    next_sums(sums, loaders(f), g, moved, f_out, g_out, parts)


def last_step_kernel(sums, f, g, out):
    step = step_length(sums)
    for z in range(PLANES):
        out[z] = f[1 + z, :ROWS] - step * g[z, :ROWS]


def call(kernel, shapes, args, scratch=(), flops=0, fetched=0, room=16):
    shapes = [jax.ShapeDtypeStruct(shape, dtype) for shape, dtype in shapes]
    moved = sum(a.size * a.dtype.itemsize for a in list(args) + shapes)
    out = pl.pallas_call(
        kernel,
        out_shape=shapes,
        in_specs=[VMEM] * (len(args) - fetched) + [pl.BlockSpec(memory_space=pltpu.HBM)] * fetched,
        out_specs=[VMEM] * len(shapes),
        scratch_shapes=list(scratch),
        compiler_params=pltpu.CompilerParams(vmem_limit_bytes=room * 1024 * 1024),
        cost_estimate=pl.CostEstimate(flops=flops, bytes_accessed=moved, transcendentals=0),
    )(*args)
    return out


def per_device(
    volume, measured, row_norm, col_norm, ray_weight, tiles, tile_kind, tile_band, band_start
):
    slabs, blocks = lax.axis_size("gz"), lax.axis_size("gy")
    block = lax.axis_index("gy")
    other_chip = [(i, i ^ 2) for i in range(blocks)]
    other_core = [(i, i ^ 1) for i in range(blocks)]
    flat = volume.reshape(PLANES * ROWS, WIDTH)
    weight = jnp.swapaxes(ray_weight, 0, 1)
    kinds, bands = jnp.swapaxes(tile_kind, 0, 1), jnp.swapaxes(tile_band, 0, 1)
    small = jnp.concatenate([(kinds + NK * bands).astype(F32), weight], axis=0)

    away = jnp.where(block >= 2, 0, (XT - REACH) * TILE)
    to_chip = lax.dynamic_slice_in_dim(flat, away, REACH * TILE, axis=1)
    to_chip, flat_later, weight_later = lax.optimization_barrier((to_chip, flat, weight))
    far = lax.ppermute(to_chip, "gy", other_chip)
    beside = block ^ 1
    window = beside * 2 + jnp.where(beside >= 2, 2, 0)
    columns = lax.dynamic_slice_in_dim(flat_later, window * TILE, WINDOW * TILE, axis=1)
    near = lax.ppermute(columns, "gy", other_core)
    w_near, w_far, w_farnear = (
        lax.ppermute(weight_later, "gy", [(i, i ^ flip) for i in range(blocks)]) for flip in (1, 2, 3)
    )
    far, near, small, w_near, w_far, w_farnear = lax.optimization_barrier(
        (far, near, small, w_near, w_far, w_farnear)
    )
    farnear = lax.ppermute(far, "gy", other_core)
    half = HALO // 2
    to_before = jnp.concatenate([volume[:, :half], col_norm[:, :half]], axis=1)
    to_after = jnp.concatenate([volume[:, ROWS - half :], col_norm[:, ROWS - half :]], axis=1)
    after = lax.ppermute(to_before, "gy", [(i + 1, i) for i in range(blocks - 1)])
    before = lax.ppermute(to_after, "gy", [(i, i + 1) for i in range(blocks - 1)])

    rows = PLANES * ANGLES
    chunk = ANGLES * QUARTER * PLANES
    slab_proj, weights = call(
        project_kernel,
        [((chunk, TILE), F32), ((EXT, ANGLES), F32)],
        (far, farnear, near, w_far, w_farnear, w_near, small, flat, tiles),
        [
            pltpu.VMEM((PLANES * ROWS, WINDOW * TILE), F32),
            pltpu.VMEM((rows, WINDOW * TILE), F32),
            pltpu.VMEM((WINDOW * 2 * rows, SLOTS * TILE), BF16),
            pltpu.VMEM((SLOTS, TILE, 2 * TILE), BF16),
            pltpu.VMEM((WINDOW * 2 * rows, 2 * TILE), F32),
            pltpu.VMEM((QUARTER, rows, TILE), F32),
            pltpu.SemaphoreType.DMA((3,)),
        ],
        fetched=2,
        room=40,
        flops=2 * WINDOW * 2 * rows * SLOTS * TILE * 2 * TILE,
    )
    chunks = slab_proj.reshape(slabs, XT, TILE)
    owner_rows = lax.all_to_all(chunks, "gz", split_axis=0, concat_axis=0, tiled=True)
    owner_rows, after, before = lax.optimization_barrier((owner_rows, after, before))
    residual, band_resid = call(
        residual_kernel,
        [(measured.shape[1:], F32), ((chunk, TILE), BF16)],
        (owner_rows.reshape(chunk, TILE), measured[0], row_norm[0], band_start),
        [pltpu.VMEM((rows, QUARTER * TILE), F32), pltpu.VMEM((chunk, TILE), F32)],
        flops=2 * 4 * rows * rows * QUARTER * TILE,
    )
    chunks = band_resid.reshape(slabs, XT, TILE)
    held = lax.all_to_all(chunks, "gz", split_axis=0, concat_axis=0, tiled=True)
    held = held.reshape(chunk, TILE)
    held_far = lax.ppermute(held, "gy", other_chip)
    held_near = lax.ppermute(held, "gy", other_core)
    held_farnear = lax.ppermute(held_far, "gy", other_core)

    ends = ((2 * (EXT + ROWS) + HALO, WIDTH), BF16)
    f, first, last, far_end, moved = call(
        back_kernel,
        [((PLANES, EXT, WIDTH), F32), ends, ends, ends, ((8, TILE), F32)],
        (
            held, held_near, held_far, held_farnear, small, weights,
            jnp.swapaxes(tiles, 1, 2), volume, col_norm, after, before,
        ),
        [
            pltpu.VMEM((chunk, TILE), F32),
            pltpu.VMEM((XT, rows, TILE), BF16),
            pltpu.VMEM((XT * rows, SLOTS * TILE), BF16),
            pltpu.VMEM((SLOTS, TILE, 2 * TILE), BF16),
            pltpu.VMEM((XT * rows, 2 * TILE), F32),
            pltpu.VMEM(volume.shape, F32),
            pltpu.VMEM(volume.shape, F32),
            pltpu.VMEM(after.shape, F32),
            pltpu.VMEM(before.shape, F32),
            pltpu.SemaphoreType.DMA((6,)),
        ],
        fetched=4,
        room=46,
        flops=2 * XT * rows * SLOTS * TILE * 2 * TILE,
    )
    pairs = [(i, i + 1) for i in range(slabs - 1)]
    within = [(i, j) for i, j in pairs if j % CHIP_ROW]
    across = [(i, j) for i, j in pairs if j % CHIP_ROW == 0]
    far_end = lax.ppermute(far_end, "gz", across + [(j, i) for i, j in across])
    below = lax.ppermute(last, "gz", within)
    above = lax.ppermute(first, "gz", [(j, i) for i, j in within])

    def exchanged(parts):
        return lax.all_to_all(parts, ("gz", "gy"), split_axis=0, concat_axis=0, tiled=True)

    partial = ((slabs * blocks, TILE), F32)
    block_ext = ((PLANES, EXT, WIDTH), F32)
    work = 40 * EXT * WIDTH
    g, parts = call(
        first_sums_kernel,
        [block_ext, partial],
        (far_end, f, below, above, moved),
        [pltpu.VMEM((1, EXT, WIDTH), F32), pltpu.VMEM((1, EXT, WIDTH), F32)],
        flops=work * PLANES,
    )
    f, g, parts = call(
        second_sums_kernel,
        [((PLANES + 4, EXT, WIDTH), F32), block_ext, partial],
        (exchanged(parts), moved, f, below, above, far_end, g),
        [pltpu.VMEM((PASSES, EXT, WIDTH), F32), pltpu.VMEM((PASSES, EXT, WIDTH), F32)],
        flops=work * (2 * PLANES + 4),
    )
    f, g, parts = call(
        third_sums_kernel,
        [((PLANES + 2, EXT, WIDTH), F32), block_ext, partial],
        (exchanged(parts), moved, f, g),
        flops=work * (2 * PLANES + 2),
    )
    (smoothed,) = call(
        last_step_kernel, [(volume.shape, F32)], (exchanged(parts), f, g), flops=2 * volume.size
    )
    return smoothed, residual[None]


def solution(mesh):
    placed = (
        P("gz", "gy", None),
        P("gz", None, "gy"),
        P("gz", None, "gy"),
        P("gz", "gy", None),
        P(None, "gy"),
        P(),
        P(),
        P(),
        P(),
    )
    return jax.shard_map(
        per_device,
        mesh=mesh,
        in_specs=placed,
        out_specs=(P("gz", "gy", None), P("gz", None, "gy")),
        check_vma=False,
    )
```
